32 devices in a mesh: section: 2 (over core), seq: 8 (over z, x), wshard: 2 (over y).
Axes of the slice: x: 2, y: 2, z: 4, core: 2. Of those that a mesh axis runs over, the one named last changes fastest.
Arguments:
- inputs: bfloat16 [2, 2, 2048, 1024], P(None, 'wshard', 'seq'), may hold values from -6 to 6
- cotangent: bfloat16 [2, 2, 2048, 1024], P(None, 'wshard', 'seq'), may hold values from -6 to 6
- boundary: int32 [2, 2], P(None, 'wshard'), may hold values from 1024 to 2048, as said below
- norm_gain: float32 [2, 1024], P('section', 'wshard'), may hold values from 0.1 to 1.9
- w_in: bfloat16 [2, 1024, 4384], P('section', 'wshard'), may hold values from -0.1875 to 0.1875
- conv_w: float32 [2, 4, 2304], P('section', None, 'wshard'), may hold values from -3 to 3
- conv_b: float32 [2, 2304], P('section', 'wshard'), may hold values from -3 to 3
- dt_bias: float32 [2, 32], P('section', 'wshard'), may hold values from -5 to -3
- a_log: float32 [2, 32], P('section', 'wshard'), may hold values from -12 to 1
- skip_gain: float32 [2, 32], P('section', 'wshard'), may hold values from 0.5 to 1.5
- gate_norm: float32 [2, 2048], P('section', 'wshard'), may hold values from 0.1 to 1.9
- w_out: bfloat16 [2, 2048, 1024], P('section', 'wshard'), may hold values from -0.125 to 0.125
Outputs:
- acts: bfloat16 [2, 2, 2, 2048, 1024], P('section', None, 'wshard', 'seq')
- in_grad: float32 [2, 2, 2, 2048, 1024], P('section', None, 'wshard', 'seq')
- grad_norm_gain: float32 [2, 1024], P('section', 'wshard')
- grad_w_in: float32 [2, 1024, 4384], P('section', 'wshard')
- grad_conv_w: float32 [2, 4, 2304], P('section', None, 'wshard')
- grad_conv_b: float32 [2, 2304], P('section', 'wshard')
- grad_dt_bias: float32 [2, 32], P('section', 'wshard')
- grad_a_log: float32 [2, 32], P('section', 'wshard')
- grad_skip_gain: float32 [2, 32], P('section', 'wshard')
- grad_gate_norm: float32 [2, 2048], P('section', 'wshard')
- grad_w_out: float32 [2, 2048, 1024], P('section', 'wshard')
The draws below stay inside these ranges and needn't reach their ends.
Inputs may be any that keep to these rules, and one draw needn't show every extreme that they name: `boundary`: for every stream index one micro-batch, drawn from the seed, holds one sequence of 2048 tokens and has the value 2048; every other holds two sequences, the second starting at the given position.
All inputs are finite; a program needn't handle non-finite values.
Results may differ from the reference program's by a relative error of at most 0.015.
The reference program's roundings to bfloat16 on the way count: a program that leaves them out, or rounds other values in their place, can miss the bound.
Values may be sent and summed in bfloat16 or wider, within the bound.
No kernel may reach another device: no remote copies, remote signals or barrier semaphores. Data moves between devices by JAX's collectives and lax.ppermute only.
A program may use at most 320 MiB of HBM per device.

```python
import math
import jax
import jax.numpy as jnp
from jax import lax

D = 1024
DI = 2048
H = 32
N = 128
K = 4
CH = 256
MB = 2
MINLEN = 1024
DPROJ = 4384
DCONV = 2304
STREAM = 2048
NW = 2
N_SECTION = 2


def draw_boundary(key, part):
    key = jax.random.fold_in(key, 11)
    key_single, key_cut = jax.random.split(key)
    single = jax.random.randint(key_single, (NW,), 0, MB)
    cut = jax.random.randint(key_cut, (MB, NW), MINLEN, STREAM - MINLEN + 1)
    rows_index = jnp.arange(MB)[:, None]
    return jnp.where(rows_index == single[None, :], STREAM, cut).astype(jnp.int32)


def draw_a_log(key, part):
    key = jax.random.fold_in(key, 23)
    key_pick, key_spot = jax.random.split(key)
    pick = jax.random.uniform(key_pick, (N_SECTION, H), jnp.float32)
    spot = jax.random.uniform(key_spot, (N_SECTION, H), jnp.float32)
    slow_high = math.log(2.0 / (STREAM * 0.03))
    slow_low = math.log(0.25 / (STREAM * 0.03))
    slow_values = slow_low + spot * (slow_high - slow_low)
    fast_values = math.log(0.6) + spot * (math.log(1.6) - math.log(0.6))
    values = jnp.where(pick < 0.5, slow_values, fast_values)
    return values.astype(jnp.float32)


def block_levels(stream_key, dims, pieces, least, largest):
    level, own = 1.0, jax.random.fold_in(stream_key, 6)
    for dim, blocks in pieces:
        steps = jnp.exp(jax.random.uniform(jax.random.fold_in(own, dim), (blocks,), jnp.float32, least / len(pieces), largest / len(pieces)))
        level = level * jnp.repeat(steps, dims[dim] // blocks).reshape([-1 if axis == dim else 1 for axis in range(len(dims))])
    return level


def gaussian(key, shape, deviation, bound, cuts=(), kind=jnp.bfloat16):
    level = block_levels(key, shape, cuts, -0.22, 0.18) if cuts else 1.0
    array = jax.random.normal(key, shape, jnp.float32) * deviation * level
    return jnp.minimum(jnp.maximum(array, -bound), bound).astype(kind)


def setup_inputs(seed: int = 0) -> dict:
    arg_keys = jax.random.split(jax.random.key(seed), 13)
    return {
        "inputs": gaussian(arg_keys[0], (MB, NW, STREAM, D), 1.0, 6.0, ((1, 2), (2, 8))),
        "cotangent": gaussian(arg_keys[1], (MB, NW, STREAM, D), 1.0, 6.0, ((1, 2), (2, 8))),
        "boundary": draw_boundary(jax.random.fold_in(arg_keys[12], 71), 0),
        "norm_gain": jnp.clip(1.0 + 0.18 * jax.random.normal(arg_keys[3], (N_SECTION, D), jnp.float32), 0.1, 1.9),
        "w_in": gaussian(arg_keys[4], (N_SECTION, D, DPROJ), D ** -0.5, 0.1875, ((0, 2), (1, 2))),
        "conv_w": gaussian(arg_keys[5], (N_SECTION, K, DCONV), K ** -0.5, 3.0, ((0, 2), (2, 2)), jnp.float32),
        "conv_b": gaussian(arg_keys[6], (N_SECTION, DCONV), 0.5, 3.0, ((0, 2), (1, 2)), jnp.float32),
        "dt_bias": jnp.clip(-5.0 + 2.0 * jax.random.uniform(arg_keys[7], (N_SECTION, H), jnp.float32) ** block_levels(arg_keys[7], (N_SECTION, H), ((0, 2), (1, 2)), -0.2, 0.2), -5.0, -3.0),
        "a_log": draw_a_log(jax.random.fold_in(arg_keys[12], 71), 0),
        "skip_gain": jnp.clip(0.5 + 1.0 * jax.random.uniform(arg_keys[9], (N_SECTION, H), jnp.float32) ** block_levels(arg_keys[9], (N_SECTION, H), ((0, 2), (1, 2)), -0.2, 0.2), 0.5, 1.5),
        "gate_norm": jnp.clip(1.0 + 0.18 * jax.random.normal(arg_keys[10], (N_SECTION, DI), jnp.float32), 0.1, 1.9),
        "w_out": gaussian(arg_keys[11], (N_SECTION, DI, D), DI ** -0.5, 0.125, ((0, 2), (1, 2))),
    }


EPSILON = 1e-05

@jax.custom_vjp
def low(v):
    return lax.optimization_barrier(v.astype(jnp.bfloat16)).astype(jnp.float32)

@jax.custom_vjp
def low_back(v):
    return v

def low_keep(v):
    return (low(v), None)

def low_pass(kept, grad):
    return (grad,)

def back_keep(v):
    return (v, None)

def back_low(kept, grad):
    return (low(grad),)
low.defvjp(low_keep, low_pass)
low_back.defvjp(back_keep, back_low)

def rms_scale(values, gain):
    mean_square = lax.optimization_barrier(jnp.mean(values * values, axis=-1, keepdims=True))
    return values * lax.rsqrt(mean_square + EPSILON) * gain

def group_step(carried, block_in):
    state_now, last_segment, running = carried
    inner_x, in_b, out_c, step_size, log_decay, segment = block_in
    cumulated = jnp.cumsum(log_decay, axis=0)
    length = segment.shape[0]
    places = jnp.arange(length)
    within = (places[:, None] >= places[None, :]) & (segment[:, None] == segment[None, :])
    spread = cumulated[:, None, :] - cumulated[None, :, :]
    decays = jnp.where(within[:, :, None], jnp.exp(jnp.where(within[:, :, None], spread, 0.0)), 0.0)
    scores = jnp.dot(out_c, in_b.T, precision=lax.Precision.HIGHEST)
    scaled_x = inner_x * step_size[:, :, None]
    output = jnp.einsum('tsh,shp->thp', decays * scores[:, :, None], scaled_x, precision=lax.Precision.HIGHEST)
    entering = jnp.exp(cumulated) * (segment == last_segment).astype(jnp.float32)[:, None]
    output = output + entering[:, :, None] * jnp.einsum('tn,hpn->thp', out_c, state_now, precision=lax.Precision.HIGHEST)
    to_end = jnp.where((segment == segment[-1])[:, None], jnp.exp(cumulated[-1][None, :] - cumulated), 0.0)
    new_state = entering[-1][:, None, None] * state_now + jnp.einsum('sh,sn,shp->hpn', to_end, in_b, scaled_x, precision=lax.Precision.HIGHEST)
    return ((new_state, segment[-1], running * entering[-1]), (output, running[None, :] * entering))

def ssd_scan(inner_x, in_b, out_c, step_size, log_decay, segment, first_state, last_segment):
    summed = inner_x.shape[0]
    blocks_count = summed // CH

    def split_blocks(array_in):
        return array_in.reshape((blocks_count, CH) + array_in.shape[1:])
    start_carry = (first_state, last_segment, jnp.ones((inner_x.shape[1],), jnp.float32))
    ending, (outputs, reach) = lax.scan(jax.checkpoint(group_step), start_carry, tuple((split_blocks(array_in) for array_in in (inner_x, in_b, out_c, step_size, log_decay, segment))))
    return (outputs.reshape(inner_x.shape), ending[0], reach.reshape(summed, inner_x.shape[1]))

def mixer_inputs(conv_pre, dt_raw, dt_bias, a_log):
    activated = jax.nn.silu(conv_pre)
    inner_x = activated[:, :DI].reshape(activated.shape[0], H, DI // H)
    in_b = activated[:, DI:DI + N]
    out_c = activated[:, DI + N:]
    step_size = jax.nn.softplus(dt_raw + dt_bias)
    log_decay = -step_size * jnp.exp(a_log)
    return (inner_x, in_b, out_c, step_size, log_decay)

def conv_piece(extended, conv_w, conv_b, tap_masks):
    length = extended.shape[0] - (K - 1)
    summed = conv_b[None, :]
    for tap_index in range(K):
        summed = summed + conv_w[tap_index][None, :] * extended[tap_index:tap_index + length] * tap_masks[tap_index][:, None]
    return summed

def mamba_layer(hidden, boundary_at, params):
    norm_gain, w_in, conv_w, conv_b, dt_bias, a_log, skip_gain, gate_norm, w_out = params
    summed = hidden.shape[0]
    normed = low(rms_scale(hidden, norm_gain))
    projected = low_back(jnp.dot(normed, w_in, precision=lax.Precision.HIGHEST))
    gate_raw = projected[:, :DI]
    conv_in = projected[:, DI:DI + DCONV]
    dt_raw = projected[:, DI + DCONV:]
    positions = jnp.arange(summed, dtype=jnp.int32)
    segment = (positions >= boundary_at).astype(jnp.float32)
    tap_masks = jnp.stack([((positions - (K - 1 - tap_index) >= boundary_at) == (positions >= boundary_at)).astype(jnp.float32) for tap_index in range(K)])
    extended = jnp.concatenate([jnp.zeros((K - 1, DCONV), jnp.float32), conv_in], axis=0)
    conv_pre = conv_piece(extended, conv_w, conv_b, tap_masks)
    inner_x, in_b, out_c, step_size, log_decay = mixer_inputs(conv_pre, dt_raw, dt_bias, a_log)
    zero_state = jnp.zeros((H, DI // H, N), jnp.float32)
    output, unused_state, unused_reach = ssd_scan(inner_x, in_b, out_c, step_size, log_decay, segment, zero_state, jnp.float32(0.0))
    mixed = (output + skip_gain[None, :, None] * inner_x).reshape(summed, DI)
    gated = low(rms_scale(mixed * jax.nn.silu(gate_raw), gate_norm))
    return hidden + jnp.dot(gated, w_out, precision=lax.Precision.HIGHEST)

def reference(inputs, cotangent, boundary, norm_gain, w_in, conv_w, conv_b, dt_bias, a_log, skip_gain, gate_norm, w_out):
    weights = tuple((array_in.astype(jnp.float32) for array_in in (norm_gain, w_in, conv_w, conv_b, dt_bias, a_log, skip_gain, gate_norm, w_out)))
    first_params = tuple((member[0] for member in weights))
    second_params = tuple((member[1] for member in weights))
    streams = inputs.reshape(-1, STREAM, D)
    cot_streams = cotangent.reshape(-1, STREAM, D)
    limits = boundary.reshape(-1).astype(jnp.int32)

    def per_stream(totals, stream_item):
        source, cot_low, boundary_at = stream_item
        source_full = source.astype(jnp.float32)

        def forward(start_in, probe_in, params_one, params_two):
            middle = low_back(low(mamba_layer(start_in, boundary_at, params_one)) + probe_in)
            return (middle, mamba_layer(middle, boundary_at, params_two))
        (middle, ending), pull_back = jax.vjp(forward, source_full, jnp.zeros_like(source_full), first_params, second_params)
        grad_start, grad_probe, grad_one, grad_two = pull_back((jnp.zeros_like(middle), cot_low.astype(jnp.float32)))
        totals = jax.tree.map(lambda running, update: running + update, totals, (grad_one, grad_two))
        return (totals, (middle.astype(jnp.bfloat16), ending.astype(jnp.bfloat16), grad_start, grad_probe))
    zero_totals = jax.tree.map(jnp.zeros_like, (first_params, second_params))
    totals, (middles, endings, grad_starts, grad_probes) = lax.scan(per_stream, zero_totals, (streams, cot_streams, limits))
    full_shape = (MB, NW, STREAM, D)
    acts = jnp.stack([middles.reshape(full_shape), endings.reshape(full_shape)])
    in_grad = jnp.stack([grad_starts.reshape(full_shape), grad_probes.reshape(full_shape)])
    stacked = [jnp.stack([one_grad, two_grad]) for one_grad, two_grad in zip(totals[0], totals[1])]
    return (acts, in_grad, stacked[0], stacked[1], stacked[2], stacked[3], stacked[4], stacked[5], stacked[6], stacked[7], stacked[8])
```

```python
import jax
import jax.numpy as jnp
from jax import lax
from jax.experimental import pallas as pl
from jax.experimental.pallas import tpu as pltpu
from jax.sharding import PartitionSpec as P

D = 1024
DI = 2048
H = 32
HEAD = DI // H
N = 128
K = 4
DCONV = 2304
DCD = DCONV + H
PAIR = 2 * HEAD
WIDE = 512
BLOCK = 256
EDGE = 8
MESSAGE = DI + 128
EPSILON = 1e-05
LOG2E = 1.4426950408889634
FAR = -1e30
F32 = jnp.float32
BF16 = jnp.bfloat16
HIGH = lax.Precision.HIGHEST


def dot(a, b):
    return jnp.dot(a, b, preferred_element_type=F32)


def dot_nt(a, b):
    return lax.dot_general(a, b, (((1,), (1,)), ((), ())), preferred_element_type=F32)


def dot_tn(a, b):
    return lax.dot_general(a, b, (((0,), (0,)), ((), ())), preferred_element_type=F32)


def iota(shape, dim):
    return lax.broadcasted_iota(jnp.int32, shape, dim)


def ones_where(condition):
    return jnp.where(condition, 1.0, 0.0).astype(F32)


def two_parts(values):
    high = values.astype(BF16)
    return high, (values - high.astype(F32)).astype(BF16)


def spread(values, start, width):
    pick = ones_where((start + iota((H, width), 1)) // HEAD == iota((H, width), 0)).astype(BF16)
    high, low = two_parts(values)
    return dot(high, pick) + dot(low, pick)


def head_sums(values, start):
    width = values.shape[1]
    pick = ones_where((start + iota((width, H), 0)) // HEAD == iota((width, H), 1)).astype(BF16)
    high, low = two_parts(values)
    return dot(high, pick) + dot(low, pick)


def sigmoid(values):
    return 0.5 * jnp.tanh(0.5 * values) + 0.5


def rows_of_one(row):
    return jnp.broadcast_to(row, (EDGE, row.shape[1]))


def segments(place, rows):
    offset, bound = place[0], place[1]
    position = offset + iota((rows, 1), 0)
    segment = ones_where(position >= bound)
    before = jnp.where(offset - 1 >= bound, 1.0, 0.0).astype(F32)
    last = jnp.where(offset + rows - 1 >= bound, 1.0, 0.0).astype(F32)
    return position, segment, before, last


def tap_masks(place, position):
    bound = place[1]
    return [
        ones_where((position - back >= bound) == (position >= bound)) if back else None
        for back in range(K)
    ]


def decay_lanes(through):
    high, low = two_parts(jnp.broadcast_to(through, (N, H)))
    first = ones_where(iota((H, 128), 0) == iota((H, 128), 1)).astype(BF16)
    second = ones_where(iota((H, 128), 0) + H == iota((H, 128), 1)).astype(BF16)
    return (dot(high, first) + dot(low, second)).astype(BF16)


def states_kernel(place, cd, edge, conv_w, conv_b, dt_bias, a_log, pre, act, step, cum, message):
    rows = cd.shape[0]
    position, segment, before, last = segments(place, rows)
    masks = tap_masks(place, position)
    step_now = jax.nn.softplus(cd[:, DCONV:] + dt_bias[...])
    log_decay = -step_now * jnp.exp(a_log[...])
    lower = ones_where(iota((rows, rows), 0) >= iota((rows, rows), 1))
    summed = jnp.dot(lower, log_decay, precision=HIGH, preferred_element_type=F32)
    step[...] = step_now
    cum[...] = summed
    total = summed[rows - 1 :, :]
    weight = step_now * jnp.where(segment == last, jnp.exp(total - summed), 0.0)
    for start in range(0, DCONV, BLOCK):
        here = slice(start, start + BLOCK)
        values = cd[:, here]
        extended = jnp.concatenate([edge[:, here], values], axis=0)
        conv = conv_b[:, here] + conv_w[K - 1 : K, here] * values
        for back in range(1, K):
            moved = pltpu.roll(extended, back, 0)[EDGE:]
            conv = conv + conv_w[K - 1 - back : K - back, here] * moved * masks[back]
        pre[:, here] = conv
        act[:, here] = conv * sigmoid(conv)
    in_t = jnp.transpose(act[:, DI : DI + N]).astype(BF16)
    for start in range(0, DI, WIDE):
        here = slice(start, start + WIDE)
        scaled = act[:, here] * spread(weight, start, WIDE)
        message[:, here] = dot(in_t, scaled.astype(BF16)).astype(BF16)
    through = jnp.exp(total) * jnp.where(before == last, 1.0, 0.0)
    message[:, DI:] = decay_lanes(through)


def carry_kernel(reverse, gathered, out, *scratch):
    count, rows = gathered.shape[0], gathered.shape[1]
    pick = ones_where(iota((2 * H, DI), 1) // HEAD == iota((2 * H, DI), 0) % H).astype(BF16)
    state = jnp.zeros((rows, DI), F32)
    for source in range(count - 1, -1, -1) if reverse else range(count):
        out[source] = state.astype(BF16)
        part = gathered[source]
        state = dot(part[:, DI : DI + 2 * H], pick) * state + part[:, :DI].astype(F32)


def intra_kernel(place, act, step, cum, skip, local):
    rows = act.shape[0]
    position, segment, _, _ = segments(place, rows)
    in_b = act[:, DI : DI + N].astype(BF16)
    out_c = act[:, DI + N :].astype(BF16)
    scores = dot_nt(out_c, in_b)
    across = place[0] + iota((1, rows), 1)
    same = segment == ones_where(across >= place[1])
    bias = jnp.where((position >= across) & same, 0.0, FAR)
    level = cum[...] * LOG2E
    level_t = jnp.transpose(level)
    steps = step[...]
    skips = rows_of_one(skip[...])
    left = iota((rows, PAIR), 1) < HEAD
    for pair in range(H // 2):
        start = pair * PAIR
        here = slice(start, start + PAIR)
        values = act[:, here]
        scaled = (values * spread(steps, start, PAIR)).astype(BF16)
        outs = []
        for head in (2 * pair, 2 * pair + 1):
            decay = jnp.exp2(level[:, head : head + 1] - level_t[head : head + 1, :] + bias)
            outs.append(dot((decay * scores).astype(BF16), scaled))
        local[:, here] = jnp.where(left, outs[0], outs[1]) + spread(skips, start, PAIR)[:1] * values


def gate_kernel(place, entry, local, act, cum, gate, gain, mixed, gated, kept):
    rows = act.shape[0]
    _, segment, before, _ = segments(place, rows)
    enter = jnp.exp(cum[...]) * ones_where(segment == before)
    out_c = act[:, DI + N :].astype(BF16)
    square = jnp.zeros((rows, 1), F32)
    for start in range(0, DI, WIDE):
        here = slice(start, start + WIDE)
        y = local[:, here] + dot(out_c, entry[:, here]) * spread(enter, start, WIDE)
        mixed[:, here] = y
        raw = gate[:, here]
        u = y * raw * sigmoid(raw)
        kept[:, here] = u
        square = square + jnp.sum(u * u, axis=1, keepdims=True)
    scale = lax.rsqrt(square / DI + EPSILON)
    for start in range(0, DI, WIDE):
        here = slice(start, start + WIDE)
        gated[:, here] = (kept[:, here] * scale * gain[:, here]).astype(BF16)


def gate_back_kernel(
    place, grad_gated, mixed, gate, gain, cum, act, grad_mixed, grad_gate, grad_gain, message, kept
):
    rows = act.shape[0]
    _, segment, before, last = segments(place, rows)
    summed = cum[...]
    enter = jnp.exp(summed) * ones_where(segment == before)
    out_t = jnp.transpose(act[:, DI + N :]).astype(BF16)
    square = jnp.zeros((rows, 1), F32)
    cross = jnp.zeros((rows, 1), F32)
    for start in range(0, DI, WIDE):
        here = slice(start, start + WIDE)
        raw = gate[:, here]
        u = mixed[:, here] * raw * sigmoid(raw)
        kept[:, here] = u
        square = square + jnp.sum(u * u, axis=1, keepdims=True)
        cross = cross + jnp.sum(grad_gated[:, here] * gain[:, here] * u, axis=1, keepdims=True)
    scale = lax.rsqrt(square / DI + EPSILON)
    pulled = scale * scale * scale * cross / DI
    for start in range(0, DI, WIDE):
        here = slice(start, start + WIDE)
        raw = gate[:, here]
        u = kept[:, here]
        up = grad_gated[:, here]
        grad_gain[:, here] = jnp.sum(up * u * scale, axis=0, keepdims=True)
        grad_u = scale * up * gain[:, here] - pulled * u
        curve = sigmoid(raw)
        grad_y = grad_u * raw * curve
        grad_gate[:, here] = (
            grad_u * mixed[:, here] * curve * (1.0 + raw * (1.0 - curve))
        ).astype(BF16)
        grad_mixed[:, here] = grad_y
        pull = (grad_y * spread(enter, start, WIDE)).astype(BF16)
        message[:, here] = dot(out_t, pull).astype(BF16)
    through = jnp.exp(summed[rows - 1 :, :]) * jnp.where(before == last, 1.0, 0.0)
    message[:, DI:] = decay_lanes(through)


def intra_back_kernel(
    place, act, step, cum, grad_mixed, entry, grad_scaled, grad_bc, grad_cum, grad_scores, across_sum
):
    rows = act.shape[0]
    position, segment, before, _ = segments(place, rows)
    in_b = act[:, DI : DI + N].astype(BF16)
    out_c = act[:, DI + N :].astype(BF16)
    scores = dot_nt(in_b, out_c)
    across = place[0] + iota((1, rows), 1)
    same = segment == ones_where(across >= place[1])
    bias = jnp.where((across >= position) & same, 0.0, FAR)
    summed = cum[...]
    level = summed * LOG2E
    level_t = jnp.transpose(level)
    steps = step[...]
    left = iota((rows, PAIR), 1) < HEAD
    lane = iota((rows, H), 1)
    grad_scores[...] = jnp.zeros((rows, rows), F32)
    down_sum = jnp.zeros((rows, H), F32)
    for pair in range(H // 2):
        start = pair * PAIR
        here = slice(start, start + PAIR)
        scaled = act[:, here] * spread(steps, start, PAIR)
        up = grad_mixed[:, here].astype(BF16)
        outs = []
        for head in (2 * pair, 2 * pair + 1):
            mine = left if head % 2 == 0 else jnp.logical_not(left)
            grad_weight = dot_nt(jnp.where(mine, scaled, 0.0).astype(BF16), up)
            decay = jnp.exp2(level_t[head : head + 1, :] - level[:, head : head + 1] + bias)
            weight = decay * scores
            grad_scores[...] += decay * grad_weight
            flow = weight * grad_weight
            across_sum[head : head + 1, :] = jnp.sum(flow, axis=0, keepdims=True)
            down_sum = down_sum + jnp.where(lane == head, jnp.sum(flow, axis=1, keepdims=True), 0.0)
            outs.append(dot(weight.astype(BF16), up))
        grad_scaled[:, here] = jnp.where(left, outs[0], outs[1])
    enter = jnp.exp(summed) * ones_where(segment == before)
    grad_out = jnp.zeros((rows, N), F32)
    grad_enter = jnp.zeros((rows, H), F32)
    for start in range(0, DI, WIDE):
        here = slice(start, start + WIDE)
        entered = entry[:, here]
        pull = grad_mixed[:, here] * spread(enter, start, WIDE)
        grad_out = grad_out + dot_nt(pull.astype(BF16), entered)
        grad_enter = grad_enter + head_sums(pull * dot(out_c, entered), start)
    low = grad_scores[...].astype(BF16)
    grad_bc[:, :N] = dot(low, out_c)
    grad_bc[:, N:] = grad_out + dot(jnp.transpose(grad_scores[...]).astype(BF16), in_b)
    grad_cum[...] = jnp.transpose(across_sum[...]) - down_sum + grad_enter


def finish_kernel(
    place,
    cd,
    edge,
    pre,
    act,
    step,
    cum,
    grad_mixed,
    grad_scaled,
    grad_bc,
    grad_cum,
    entry,
    leaving,
    conv_w,
    dt_bias,
    a_log,
    skip,
    grad_cd,
    grad_tail,
    grad_edge,
    grad_conv_w,
    grad_conv_b,
    grad_heads,
    grad_pre,
):
    rows = cd.shape[0]
    position, segment, before, last = segments(place, rows)
    masks = tap_masks(place, position)
    summed = cum[...]
    total = summed[rows - 1 :, :]
    to_end = jnp.where(segment == last, jnp.exp(total - summed), 0.0)
    steps = step[...]
    skips = rows_of_one(skip[...])
    in_b = act[:, DI : DI + N].astype(BF16)

    def silu_slope(values):
        curve = sigmoid(values)
        return curve * (1.0 + values * (1.0 - curve))

    grad_end = jnp.zeros((rows, H), F32)
    grad_step = jnp.zeros((rows, H), F32)
    grad_in = grad_bc[:, :N]
    grad_through = jnp.zeros((EDGE, H), F32)
    grad_skip = jnp.zeros((EDGE, H), F32)
    for start in range(0, DI, WIDE):
        here = slice(start, start + WIDE)
        values = act[:, here]
        up = grad_mixed[:, here]
        left = leaving[:, here]
        step_wide = spread(steps, start, WIDE)
        end_wide = spread(to_end, start, WIDE)
        pulled = dot(in_b, left) * end_wide
        scaled = values * step_wide
        grad_now = grad_scaled[:, here] + pulled
        grad_end = grad_end + head_sums(scaled * pulled, start)
        grad_step = grad_step + head_sums(grad_now * values, start)
        grad_in = grad_in + dot_nt((end_wide * scaled).astype(BF16), left)
        states = jnp.sum(entry[:, here].astype(F32) * left.astype(F32), axis=0, keepdims=True)
        grad_through = grad_through + head_sums(rows_of_one(states), start)
        skipped = jnp.sum(up * values, axis=0, keepdims=True)
        grad_skip = grad_skip + head_sums(rows_of_one(skipped), start)
        grad_x = grad_now * step_wide + spread(skips, start, WIDE)[:1] * up
        grad_pre[:, here] = grad_x * silu_slope(pre[:, here])
    grad_pre[:, DI : DI + N] = grad_in * silu_slope(pre[:, DI : DI + N])
    grad_pre[:, DI + N :] = grad_bc[:, N:] * silu_slope(pre[:, DI + N :])
    through = jnp.exp(total) * jnp.where(before == last, 1.0, 0.0)
    at_last = jnp.sum(grad_end, axis=0, keepdims=True) + through * grad_through[:1]
    upper = ones_where(iota((rows, rows), 1) >= iota((rows, rows), 0))
    grad_log = at_last + jnp.dot(
        upper, grad_cum[...] - grad_end, precision=HIGH, preferred_element_type=F32
    )
    rate = jnp.exp(a_log[...])
    grad_step = grad_step - rate * grad_log
    grad_raw = grad_step * sigmoid(cd[:, DCONV:] + dt_bias[...])
    grad_cd[:, DCONV:] = grad_raw.astype(BF16)
    grad_heads[0:1, :] = jnp.sum(grad_raw, axis=0, keepdims=True)
    grad_heads[1:2, :] = jnp.sum(grad_log * -steps * rate, axis=0, keepdims=True)
    grad_heads[2:3, :] = grad_skip[:1]
    grad_heads[3:, :] = jnp.zeros((EDGE - 3, H), F32)
    nothing = jnp.zeros((EDGE, BLOCK), F32)
    for start in range(0, DCONV, BLOCK):
        here = slice(start, start + BLOCK)
        values = cd[:, here]
        extended = jnp.concatenate([edge[:, here], values], axis=0)
        up = grad_pre[:, here]
        grad_conv_b[:, here] = jnp.sum(up, axis=0, keepdims=True)
        grad_conv_w[K - 1 : K, here] = jnp.sum(up * values, axis=0, keepdims=True)
        spilled = nothing
        grad_in_now = conv_w[K - 1 : K, here] * up
        for back in range(1, K):
            moved = pltpu.roll(extended, back, 0)[EDGE:]
            masked = up * masks[back]
            grad_conv_w[K - 1 - back : K - back, here] = jnp.sum(
                masked * moved, axis=0, keepdims=True
            )
            framed = jnp.concatenate([nothing, masked, nothing], axis=0)
            returned = pltpu.roll(framed, rows + 2 * EDGE - back, 0)
            tap = conv_w[K - 1 - back : K - back, here]
            spilled = spilled + tap * returned[:EDGE]
            grad_in_now = grad_in_now + tap * returned[EDGE : EDGE + rows]
        grad_edge[:, here] = spilled
        grad_tail[:, here] = grad_in_now[rows - EDGE :]
        grad_cd[:, here] = grad_in_now.astype(BF16)


def call(body, outs, scratch, *operands):
    whole = pl.BlockSpec(memory_space=pltpu.VMEM)
    scalars = [pl.BlockSpec(memory_space=pltpu.SMEM)] if operands[0].dtype == jnp.int32 else []
    return pl.pallas_call(
        body,
        out_shape=[jax.ShapeDtypeStruct(shape, kind) for shape, kind in outs],
        in_specs=scalars + [whole] * (len(operands) - len(scalars)),
        out_specs=[whole] * len(outs),
        scratch_shapes=[pltpu.VMEM(shape, kind) for shape, kind in scratch],
        compiler_params=pltpu.CompilerParams(vmem_limit_bytes=56 * 1024 * 1024),
    )(*operands)


def turned(block, axis, distance):
    count = lax.axis_size(axis)
    return lax.ppermute(block, axis, [(i, (i + distance) % count) for i in range(count)])


def from_behind(block, axis, distance):
    devices = range(lax.axis_size(axis))
    route = [(i - distance, i) for i in devices if i - distance in devices]
    return lax.ppermute(block, axis, route)


def exchange_states(message, reverse):
    count = lax.axis_size("seq")
    rows = N // count
    sent = message.reshape(count, rows, MESSAGE)
    gathered = lax.all_to_all(sent, "seq", 0, 0)

    def body(gathered_ref, out_ref):
        carry_kernel(reverse, gathered_ref, out_ref)

    (states,) = call(body, [((count, rows, DI), BF16)], [], gathered)
    return lax.all_to_all(states, "seq", 0, 0).reshape(N, DI)


def on_device(
    inputs,
    cotangent,
    boundary,
    norm_gain,
    w_in,
    conv_w,
    conv_b,
    dt_bias,
    a_log,
    skip_gain,
    gate_norm,
    w_out,
):
    section = lax.axis_index("section")
    sections = lax.axis_size("section")
    shard = lax.axis_index("wshard")
    shards = lax.axis_size("wshard")
    batches, _, rows, _ = inputs.shape
    offset = lax.axis_index("seq") * rows

    source = lax.dynamic_index_in_dim(inputs[:, 0], section, keepdims=False)
    upstream = lax.dynamic_index_in_dim(cotangent[:, 0], section, keepdims=False)
    bound = lax.dynamic_index_in_dim(boundary[:, 0], section, keepdims=False)
    place = jnp.stack([offset, bound]).astype(jnp.int32)

    small_parts = (norm_gain, conv_w, conv_b, dt_bias, a_log, skip_gain, gate_norm)
    flat = jnp.concatenate([part.reshape(-1) for part in small_parts])
    every_small = lax.all_gather(flat, ("section", "wshard")).reshape(sections, shards, -1)

    def small_of(layer):
        out, at = [], 0
        for part in small_parts:
            size = part.size
            piece = every_small[layer, :, at : at + size]
            at += size
            piece = piece.reshape((shards,) + part.shape[1:])
            if part.ndim == 3:
                out.append(jnp.moveaxis(piece, 0, 1).reshape(part.shape[1], -1))
            else:
                out.append(piece.reshape(1, -1))
        return out

    own_blocks = (w_in[0, :, DI:], w_in[0, :, :DI], w_out[0])
    block_at = [(shard + away) % shards for away in range(shards)]
    weights = [[], []]
    for own in own_blocks:
        blocks = [own] + [turned(own, "wshard", -away) for away in range(1, shards)]
        others = [turned(block, "section", 1) for block in blocks]
        for layer in range(sections):
            weights[layer].append(
                [jnp.where(section == layer, a, b) for a, b in zip(blocks, others)]
            )

    def times(low, blocks):
        total = None
        for at, block in zip(block_at, blocks):
            size = block.shape[0]
            part = lax.dynamic_slice_in_dim(low, at * size, size, 1)
            term = jnp.dot(part, block, preferred_element_type=F32)
            total = term if total is None else total + term
        return total

    def times_back(terms, blocks):
        size = blocks[0].shape[0]
        parts = []
        for columns in range(shards):
            parts.append(
                sum(
                    lax.dot_general(
                        low, blocks_now[columns], (((1,), (1,)), ((), ())), preferred_element_type=F32
                    )
                    for low, blocks_now in terms
                )
            )
        if shards == 2:
            return jnp.where(
                shard == 0,
                jnp.concatenate(parts, axis=1),
                jnp.concatenate(parts[::-1], axis=1),
            )
        out = jnp.zeros((rows, size * shards), F32)
        for at, part in zip(block_at, parts):
            out = lax.dynamic_update_slice_in_dim(out, part, at * size, 1)
        return out

    def layer_forward(layer, hidden_low):
        w_cd, w_gate, w_last = weights[layer]
        gain_pre, taps, conv_bias, bias_dt, log_rate, skip, gain_gate = small_of(layer)
        hidden = hidden_low.astype(F32)
        scale = lax.rsqrt(jnp.mean(hidden * hidden, axis=-1, keepdims=True) + EPSILON)
        normed_low = (hidden * scale * gain_pre).astype(BF16)
        cd = times(normed_low, w_cd)
        edge = from_behind(cd[rows - EDGE :, :DCONV], "seq", 1)
        gate = times(normed_low, w_gate)
        pre, act, step, cum, message = call(
            states_kernel,
            [
                ((rows, DCONV), F32),
                ((rows, DCONV), F32),
                ((rows, H), F32),
                ((rows, H), F32),
                ((N, MESSAGE), BF16),
            ],
            [],
            place,
            cd,
            edge,
            taps,
            conv_bias,
            bias_dt,
            log_rate,
        )
        entry = exchange_states(message, False)
        (local,) = call(intra_kernel, [((rows, DI), F32)], [], place, act, step, cum, skip)
        mixed, gated_low = call(
            gate_kernel,
            [((rows, DI), F32), ((rows, DI), BF16)],
            [((rows, DI), F32)],
            place,
            entry,
            local,
            act,
            cum,
            gate,
            gain_gate,
        )
        result = (hidden + times(gated_low, w_last)).astype(BF16)
        kept = (hidden, scale, normed_low, cd, edge, gate, pre, act, step, cum, entry, mixed, gated_low)
        return result, kept

    def weight_terms(low, up):
        size = low.shape[1] // shards
        half = size // sections
        out = []
        for turn in range(sections):
            which = (section + turn) % sections
            out.append(
                [
                    lax.dot_general(
                        lax.dynamic_slice_in_dim(low, at * size + which * half, half, 1),
                        up,
                        (((0,), (0,)), ((), ())),
                        preferred_element_type=F32,
                    )
                    for at in block_at
                ]
            )
        return out

    def reduce_weight(low, up):
        terms = weight_terms(low, up)
        own = terms[0]
        for turn in range(1, sections):
            sent = [turned(block.astype(BF16), "section", turn) for block in terms[turn]]
            own = [a + b.astype(F32) for a, b in zip(own, sent)]
        total = own[0]
        for away in range(1, shards):
            total = total + turned(own[away].astype(BF16), "wshard", away).astype(F32)
        return lax.psum(total.astype(BF16), "seq")

    def layer_backward(layer, up_low, kept):
        w_cd, w_gate, w_last = weights[layer]
        gain_pre, taps, conv_bias, bias_dt, log_rate, skip, gain_gate = small_of(layer)
        hidden, scale, normed_low, cd, edge, gate, pre, act, step, cum, entry, mixed, gated_low = kept
        reduced_out = reduce_weight(gated_low, up_low)
        grad_gated = times_back([(up_low, w_last)], w_last)
        grad_mixed, grad_gate, grad_gain_gate, message = call(
            gate_back_kernel,
            [
                ((rows, DI), F32),
                ((rows, DI), BF16),
                ((1, DI), F32),
                ((N, MESSAGE), BF16),
            ],
            [((rows, DI), F32)],
            place,
            grad_gated,
            mixed,
            gate,
            gain_gate,
            cum,
            act,
        )
        leaving = exchange_states(message, True)
        reduced_gate = reduce_weight(normed_low, grad_gate)
        grad_scaled, grad_bc, grad_cum = call(
            intra_back_kernel,
            [((rows, DI), F32), ((rows, 2 * N), F32), ((rows, H), F32)],
            [((rows, rows), F32), ((H, rows), F32)],
            place,
            act,
            step,
            cum,
            grad_mixed,
            entry,
        )
        grad_cd, grad_tail, grad_edge, grad_taps, grad_conv_bias, grad_heads = call(
            finish_kernel,
            [
                ((rows, DCD), BF16),
                ((EDGE, DCONV), F32),
                ((EDGE, DCONV), F32),
                ((K, DCONV), F32),
                ((1, DCONV), F32),
                ((EDGE, H), F32),
            ],
            [((rows, DCONV), F32)],
            place,
            cd,
            edge,
            pre,
            act,
            step,
            cum,
            grad_mixed,
            grad_scaled,
            grad_bc,
            grad_cum,
            entry,
            leaving,
            taps,
            bias_dt,
            log_rate,
            skip,
        )
        edge_back = from_behind(grad_edge, "seq", -1)
        grad_cd = lax.dynamic_update_slice(
            grad_cd, (grad_tail + edge_back).astype(BF16), (rows - EDGE, 0)
        )
        grad_normed = times_back([(grad_cd, w_cd), (grad_gate, w_gate)], w_cd)
        grad_pulled = grad_normed * gain_pre
        cross = jnp.mean(grad_pulled * hidden, axis=-1, keepdims=True)
        grad_hidden = up_low.astype(F32) + scale * grad_pulled - scale**3 * cross * hidden
        grad_gain_pre = jnp.sum(grad_normed * hidden * scale, axis=0)
        reduced_cd = reduce_weight(normed_low, grad_cd)
        small = (
            grad_gain_pre,
            grad_taps,
            grad_conv_bias,
            grad_heads[0],
            grad_heads[1],
            grad_heads[2],
            grad_gain_gate,
        )
        return grad_hidden, (reduced_cd, reduced_gate, reduced_out), small

    middle, kept_first = layer_forward(0, source)
    ending, kept_second = layer_forward(1, middle)
    grad_middle, large_second, small_second = layer_backward(1, upstream, kept_second)
    grad_middle_low = grad_middle.astype(BF16)
    grad_source, large_first, small_first = layer_backward(0, grad_middle_low, kept_first)

    is_first = section == 0

    def placed(first, second):
        keep = jnp.where(is_first, first, second)
        get = turned(jnp.where(is_first, second, first), "section", 1)
        return jnp.stack([jnp.where(is_first, keep, get), jnp.where(is_first, get, keep)])

    acts = placed(middle, ending).reshape(1, batches, 1, rows, D)
    in_keep = jnp.where(is_first, grad_source, grad_middle_low.astype(F32))
    in_get = turned(
        jnp.where(is_first, grad_middle_low, grad_source.astype(BF16)), "section", 1
    ).astype(F32)
    in_grad = jnp.stack([jnp.where(is_first, in_keep, in_get), jnp.where(is_first, in_get, in_keep)])
    in_grad = in_grad.reshape(1, batches, 1, rows, D)

    def whole_weight(first, second):
        keep = jnp.where(is_first, first, second)
        get = turned(jnp.where(is_first, second, first), "section", 1)
        return jnp.where(
            is_first,
            jnp.concatenate([keep, get], axis=0),
            jnp.concatenate([get, keep], axis=0),
        ).astype(F32)

    part_cd, part_gate, part_out = [whole_weight(a, b) for a, b in zip(large_first, large_second)]
    part_in = jnp.concatenate([part_gate, part_cd], axis=1)

    flat_grads = jnp.stack(
        [jnp.concatenate([part.reshape(-1) for part in small]) for small in (small_first, small_second)]
    )
    summed_small = lax.psum(flat_grads, ("section", "seq", "wshard"))
    mine = lax.dynamic_index_in_dim(summed_small, section, keepdims=False)
    small_out, at = [], 0
    for part, shown in zip(small_first, small_parts):
        size = part.size
        piece = mine[at : at + size].reshape(part.shape)
        at += size
        width = shown.shape[-1]
        piece = lax.dynamic_slice_in_dim(piece, shard * width, width, piece.ndim - 1)
        small_out.append(piece.reshape(shown.shape))
    return (acts, in_grad, small_out[0], part_in[None], *small_out[1:], part_out[None])


def solution(mesh):
    placed = (
        P(None, "wshard", "seq", None),
        P(None, "wshard", "seq", None),
        P(None, "wshard"),
        P("section", "wshard"),
        P("section", "wshard", None),
        P("section", None, "wshard"),
        P("section", "wshard"),
        P("section", "wshard"),
        P("section", "wshard"),
        P("section", "wshard"),
        P("section", "wshard"),
        P("section", "wshard", None),
    )
    return jax.shard_map(
        on_device,
        mesh=mesh,
        in_specs=placed,
        out_specs=(
            P("section", None, "wshard", "seq", None),
            P("section", None, "wshard", "seq", None),
            P("section", "wshard"),
            P("section", "wshard", None),
            P("section", None, "wshard"),
            P("section", "wshard"),
            P("section", "wshard"),
            P("section", "wshard"),
            P("section", "wshard"),
            P("section", "wshard"),
            P("section", "wshard", None),
        ),
        check_vma=False,
    )
```

```python
import jax
import jax.numpy as jnp
from jax import lax
from jax.experimental import pallas as pl
from jax.experimental.pallas import tpu as pltpu
from jax.sharding import PartitionSpec as P

D = 1024
DI = 2048
H = 32
HEAD = DI // H
N = 128
K = 4
DCONV = 2304
DCD = DCONV + H
PAIR = 2 * HEAD
WIDE = 512
BLOCK = 256
EDGE = 8
MESSAGE = DI + 128
EPSILON = 1e-05
LOG2E = 1.4426950408889634
FAR = -1e30
F32 = jnp.float32
BF16 = jnp.bfloat16
HIGH = lax.Precision.HIGHEST


def dot(a, b):
    return jnp.dot(a, b, preferred_element_type=F32)


def dot_nt(a, b):
    return lax.dot_general(a, b, (((1,), (1,)), ((), ())), preferred_element_type=F32)


def dot_tn(a, b):
    return lax.dot_general(a, b, (((0,), (0,)), ((), ())), preferred_element_type=F32)


def iota(shape, dim):
    return lax.broadcasted_iota(jnp.int32, shape, dim)


def ones_where(condition):
    return jnp.where(condition, 1.0, 0.0).astype(F32)


def two_parts(values):
    high = values.astype(BF16)
    return high, (values - high.astype(F32)).astype(BF16)


def spread(values, start, width):
    pick = ones_where((start + iota((H, width), 1)) // HEAD == iota((H, width), 0)).astype(BF16)
    high, low = two_parts(values)
    return dot(high, pick) + dot(low, pick)


def head_sums(values, start):
    width = values.shape[1]
    pick = ones_where((start + iota((width, H), 0)) // HEAD == iota((width, H), 1)).astype(BF16)
    high, low = two_parts(values)
    return dot(high, pick) + dot(low, pick)


def sigmoid(values):
    return 0.5 * jnp.tanh(0.5 * values) + 0.5


def rows_of_one(row):
    return jnp.broadcast_to(row, (EDGE, row.shape[1]))


def segments(place, rows):
    offset, bound = place[0], place[1]
    position = offset + iota((rows, 1), 0)
    segment = ones_where(position >= bound)
    before = jnp.where(offset - 1 >= bound, 1.0, 0.0).astype(F32)
    last = jnp.where(offset + rows - 1 >= bound, 1.0, 0.0).astype(F32)
    return position, segment, before, last


def tap_masks(place, position):
    bound = place[1]
    return [
        ones_where((position - back >= bound) == (position >= bound)) if back else None
        for back in range(K)
    ]


def decay_lanes(through):
    high, low = two_parts(jnp.broadcast_to(through, (N, H)))
    first = ones_where(iota((H, 128), 0) == iota((H, 128), 1)).astype(BF16)
    second = ones_where(iota((H, 128), 0) + H == iota((H, 128), 1)).astype(BF16)
    return dot(high, first) + dot(low, second)


def states_kernel(place, cd, edge, conv_w, conv_b, dt_bias, a_log, pre, act, step, cum, message):
    rows = cd.shape[0]
    position, segment, before, last = segments(place, rows)
    masks = tap_masks(place, position)
    step_now = jax.nn.softplus(cd[:, DCONV:] + dt_bias[...])
    log_decay = -step_now * jnp.exp(a_log[...])
    lower = ones_where(iota((rows, rows), 0) >= iota((rows, rows), 1))
    summed = jnp.dot(lower, log_decay, precision=HIGH, preferred_element_type=F32)
    step[...] = step_now
    cum[...] = summed
    total = summed[rows - 1 :, :]
    weight = step_now * jnp.where(segment == last, jnp.exp(total - summed), 0.0)
    for start in range(0, DCONV, BLOCK):
        here = slice(start, start + BLOCK)
        values = cd[:, here]
        extended = jnp.concatenate([edge[:, here], values], axis=0)
        conv = conv_b[:, here] + conv_w[K - 1 : K, here] * values
        for back in range(1, K):
            moved = pltpu.roll(extended, back, 0)[EDGE:]
            conv = conv + conv_w[K - 1 - back : K - back, here] * moved * masks[back]
        pre[:, here] = conv
        act[:, here] = conv * sigmoid(conv)
    in_high, in_low = two_parts(jnp.transpose(act[:, DI : DI + N]))
    for start in range(0, DI, WIDE):
        here = slice(start, start + WIDE)
        high, low = two_parts(act[:, here] * spread(weight, start, WIDE))
        message[:, here] = dot(in_high, high) + dot(in_high, low) + dot(in_low, high)
    through = jnp.exp(total) * jnp.where(before == last, 1.0, 0.0)
    message[:, DI:] = decay_lanes(through).astype(message.dtype)


def carry_kernel(reverse, gathered, out, *scratch):
    count, rows = gathered.shape[0], gathered.shape[1]
    pick = ones_where(iota((2 * H, DI), 1) // HEAD == iota((2 * H, DI), 0) % H).astype(BF16)
    state = jnp.zeros((rows, DI), F32)
    for source in range(count - 1, -1, -1) if reverse else range(count):
        out[source] = state.astype(out.dtype)
        part = gathered[source]
        through = dot(part[:, DI : DI + 2 * H].astype(BF16), pick)
        state = through * state + part[:, :DI].astype(F32)


def intra_kernel(place, act, step, cum, skip, local):
    rows = act.shape[0]
    position, segment, _, _ = segments(place, rows)
    scores = lax.dot_general(
        act[:, DI + N :],
        act[:, DI : DI + N],
        (((1,), (1,)), ((), ())),
        precision=HIGH,
        preferred_element_type=F32,
    )
    across = place[0] + iota((1, rows), 1)
    same = segment == ones_where(across >= place[1])
    bias = jnp.where((position >= across) & same, 0.0, FAR)
    level = cum[...] * LOG2E
    level_t = jnp.transpose(level)
    steps = step[...]
    skips = rows_of_one(skip[...])
    left = iota((rows, PAIR), 1) < HEAD
    for pair in range(H // 2):
        start = pair * PAIR
        here = slice(start, start + PAIR)
        values = act[:, here]
        high, low = two_parts(values * spread(steps, start, PAIR))
        scaled = jnp.concatenate([high, low], axis=1)
        outs = []
        for head in (2 * pair, 2 * pair + 1):
            decay = jnp.exp2(level[:, head : head + 1] - level_t[head : head + 1, :] + bias)
            first, second = two_parts(decay * scores)
            both = dot(first, scaled)
            outs.append(both[:, :PAIR] + both[:, PAIR:] + dot(second, high))
        local[:, here] = jnp.where(left, outs[0], outs[1]) + spread(skips, start, PAIR)[:1] * values


def gate_kernel(place, entry, local, act, cum, gate, gain, mixed, gated, kept):
    rows = act.shape[0]
    _, segment, before, _ = segments(place, rows)
    enter = jnp.exp(cum[...]) * ones_where(segment == before)
    out_high, out_low = two_parts(act[:, DI + N :])
    square = jnp.zeros((rows, 1), F32)
    for start in range(0, DI, WIDE):
        here = slice(start, start + WIDE)
        high, low = two_parts(entry[:, here])
        entered = dot(out_high, high) + dot(out_low, high) + dot(out_high, low)
        y = local[:, here] + entered * spread(enter, start, WIDE)
        mixed[:, here] = y
        raw = gate[:, here]
        u = y * raw * sigmoid(raw)
        kept[:, here] = u
        square = square + jnp.sum(u * u, axis=1, keepdims=True)
    scale = lax.rsqrt(square / DI + EPSILON)
    count = place.shape[0] - 2
    width = DI // count
    for group in range(count):
        here = slice(group * width, (group + 1) * width)
        there = pl.ds(pl.multiple_of(place[2 + group], 128), width)
        gated[:, there] = (kept[:, here] * scale * gain[:, here]).astype(BF16)


def gate_back_kernel(
    place, grad_gated, mixed, gate, gain, cum, act, grad_mixed, grad_gate, grad_gain, message, kept
):
    rows = act.shape[0]
    _, segment, before, last = segments(place, rows)
    summed = cum[...]
    enter = jnp.exp(summed) * ones_where(segment == before)
    out_t = jnp.transpose(act[:, DI + N :]).astype(BF16)
    square = jnp.zeros((rows, 1), F32)
    cross = jnp.zeros((rows, 1), F32)
    count = place.shape[0] - 2
    width = DI // count
    for group in range(count):
        here = slice(group * width, (group + 1) * width)
        there = pl.ds(pl.multiple_of(place[2 + group], 128), width)
        raw = gate[:, here]
        u = mixed[:, here] * raw * sigmoid(raw)
        kept[:, here] = u
        square = square + jnp.sum(u * u, axis=1, keepdims=True)
        cross = cross + jnp.sum(grad_gated[:, there] * gain[:, here] * u, axis=1, keepdims=True)
    scale = lax.rsqrt(square / DI + EPSILON)
    pulled = scale * scale * scale * cross / DI
    for group in range(count):
        start = group * width
        here = slice(start, start + width)
        there = pl.ds(pl.multiple_of(place[2 + group], 128), width)
        raw = gate[:, here]
        u = kept[:, here]
        up = grad_gated[:, there]
        grad_gain[:, here] = jnp.sum(up * u * scale, axis=0, keepdims=True)
        grad_u = scale * up * gain[:, here] - pulled * u
        curve = sigmoid(raw)
        grad_y = grad_u * raw * curve
        grad_gate[:, here] = (
            grad_u * mixed[:, here] * curve * (1.0 + raw * (1.0 - curve))
        ).astype(BF16)
        grad_mixed[:, here] = grad_y
        pull = (grad_y * spread(enter, start, width)).astype(BF16)
        message[:, here] = dot(out_t, pull).astype(BF16)
    through = jnp.exp(summed[rows - 1 :, :]) * jnp.where(before == last, 1.0, 0.0)
    message[:, DI:] = decay_lanes(through).astype(message.dtype)


def intra_back_kernel(
    place, act, step, cum, grad_mixed, entry, grad_scaled, grad_bc, grad_cum, grad_scores, across_sum
):
    rows = act.shape[0]
    position, segment, before, _ = segments(place, rows)
    in_b = act[:, DI : DI + N].astype(BF16)
    out_c = act[:, DI + N :].astype(BF16)
    scores = dot_nt(in_b, out_c)
    across = place[0] + iota((1, rows), 1)
    same = segment == ones_where(across >= place[1])
    bias = jnp.where((across >= position) & same, 0.0, FAR)
    summed = cum[...]
    level = summed * LOG2E
    level_t = jnp.transpose(level)
    steps = step[...]
    left = iota((rows, PAIR), 1) < HEAD
    lane = iota((rows, H), 1)
    grad_scores[...] = jnp.zeros((rows, rows), F32)
    down_sum = jnp.zeros((rows, H), F32)
    for pair in range(H // 2):
        start = pair * PAIR
        here = slice(start, start + PAIR)
        scaled = act[:, here] * spread(steps, start, PAIR)
        up = grad_mixed[:, here].astype(BF16)
        outs = []
        for head in (2 * pair, 2 * pair + 1):
            mine = left if head % 2 == 0 else jnp.logical_not(left)
            grad_weight = dot_nt(jnp.where(mine, scaled, 0.0).astype(BF16), up)
            decay = jnp.exp2(level_t[head : head + 1, :] - level[:, head : head + 1] + bias)
            weight = decay * scores
            grad_scores[...] += decay * grad_weight
            flow = weight * grad_weight
            across_sum[head : head + 1, :] = jnp.sum(flow, axis=0, keepdims=True)
            down_sum = down_sum + jnp.where(lane == head, jnp.sum(flow, axis=1, keepdims=True), 0.0)
            outs.append(dot(weight.astype(BF16), up))
        grad_scaled[:, here] = jnp.where(left, outs[0], outs[1])
    enter = jnp.exp(summed) * ones_where(segment == before)
    grad_out = jnp.zeros((rows, N), F32)
    grad_enter = jnp.zeros((rows, H), F32)
    for start in range(0, DI, WIDE):
        here = slice(start, start + WIDE)
        entered = entry[:, here].astype(BF16)
        pull = grad_mixed[:, here] * spread(enter, start, WIDE)
        grad_out = grad_out + dot_nt(pull.astype(BF16), entered)
        grad_enter = grad_enter + head_sums(pull * dot(out_c, entered), start)
    low = grad_scores[...].astype(BF16)
    grad_bc[:, :N] = dot(low, out_c)
    grad_bc[:, N:] = grad_out + dot(jnp.transpose(grad_scores[...]).astype(BF16), in_b)
    grad_cum[...] = jnp.transpose(across_sum[...]) - down_sum + grad_enter


def finish_kernel(
    place,
    cd,
    edge,
    pre,
    act,
    step,
    cum,
    grad_mixed,
    grad_scaled,
    grad_bc,
    grad_cum,
    entry,
    leaving,
    conv_w,
    dt_bias,
    a_log,
    skip,
    grad_cd,
    grad_tail,
    grad_edge,
    grad_conv_w,
    grad_conv_b,
    grad_heads,
    grad_pre,
):
    rows = cd.shape[0]
    position, segment, before, last = segments(place, rows)
    masks = tap_masks(place, position)
    summed = cum[...]
    total = summed[rows - 1 :, :]
    to_end = jnp.where(segment == last, jnp.exp(total - summed), 0.0)
    steps = step[...]
    skips = rows_of_one(skip[...])
    in_b = act[:, DI : DI + N].astype(BF16)

    def silu_slope(values):
        curve = sigmoid(values)
        return curve * (1.0 + values * (1.0 - curve))

    grad_end = jnp.zeros((rows, H), F32)
    grad_step = jnp.zeros((rows, H), F32)
    grad_in = grad_bc[:, :N]
    grad_through = jnp.zeros((EDGE, H), F32)
    grad_skip = jnp.zeros((EDGE, H), F32)
    for start in range(0, DI, WIDE):
        here = slice(start, start + WIDE)
        values = act[:, here]
        up = grad_mixed[:, here]
        left = leaving[:, here]
        step_wide = spread(steps, start, WIDE)
        end_wide = spread(to_end, start, WIDE)
        pulled = dot(in_b, left) * end_wide
        scaled = values * step_wide
        grad_now = grad_scaled[:, here] + pulled
        grad_end = grad_end + head_sums(scaled * pulled, start)
        grad_step = grad_step + head_sums(grad_now * values, start)
        grad_in = grad_in + dot_nt((end_wide * scaled).astype(BF16), left)
        states = jnp.sum(entry[:, here].astype(F32) * left.astype(F32), axis=0, keepdims=True)
        grad_through = grad_through + head_sums(rows_of_one(states), start)
        skipped = jnp.sum(up * values, axis=0, keepdims=True)
        grad_skip = grad_skip + head_sums(rows_of_one(skipped), start)
        grad_x = grad_now * step_wide + spread(skips, start, WIDE)[:1] * up
        grad_pre[:, here] = grad_x * silu_slope(pre[:, here])
    grad_pre[:, DI : DI + N] = grad_in * silu_slope(pre[:, DI : DI + N])
    grad_pre[:, DI + N :] = grad_bc[:, N:] * silu_slope(pre[:, DI + N :])
    through = jnp.exp(total) * jnp.where(before == last, 1.0, 0.0)
    at_last = jnp.sum(grad_end, axis=0, keepdims=True) + through * grad_through[:1]
    upper = ones_where(iota((rows, rows), 1) >= iota((rows, rows), 0))
    grad_log = at_last + jnp.dot(
        upper, grad_cum[...] - grad_end, precision=HIGH, preferred_element_type=F32
    )
    rate = jnp.exp(a_log[...])
    grad_step = grad_step - rate * grad_log
    grad_raw = grad_step * sigmoid(cd[:, DCONV:] + dt_bias[...])
    grad_cd[:, DCONV:] = grad_raw.astype(BF16)
    grad_heads[0:1, :] = jnp.sum(grad_raw, axis=0, keepdims=True)
    grad_heads[1:2, :] = jnp.sum(grad_log * -steps * rate, axis=0, keepdims=True)
    grad_heads[2:3, :] = grad_skip[:1]
    grad_heads[3:, :] = jnp.zeros((EDGE - 3, H), F32)
    nothing = jnp.zeros((EDGE, BLOCK), F32)
    for start in range(0, DCONV, BLOCK):
        here = slice(start, start + BLOCK)
        values = cd[:, here]
        extended = jnp.concatenate([edge[:, here], values], axis=0)
        up = grad_pre[:, here]
        grad_conv_b[:, here] = jnp.sum(up, axis=0, keepdims=True)
        grad_conv_w[K - 1 : K, here] = jnp.sum(up * values, axis=0, keepdims=True)
        spilled = nothing
        grad_in_now = conv_w[K - 1 : K, here] * up
        for back in range(1, K):
            moved = pltpu.roll(extended, back, 0)[EDGE:]
            masked = up * masks[back]
            grad_conv_w[K - 1 - back : K - back, here] = jnp.sum(
                masked * moved, axis=0, keepdims=True
            )
            framed = jnp.concatenate([nothing, masked, nothing], axis=0)
            returned = pltpu.roll(framed, rows + 2 * EDGE - back, 0)
            tap = conv_w[K - 1 - back : K - back, here]
            spilled = spilled + tap * returned[:EDGE]
            grad_in_now = grad_in_now + tap * returned[EDGE : EDGE + rows]
        grad_edge[:, here] = spilled
        grad_tail[:, here] = grad_in_now[rows - EDGE :]
        grad_cd[:, here] = grad_in_now.astype(BF16)


def place_kernel(
    pick, gate, gate_other, late, late_other, out_and_cd, out_and_cd_other, second, second_other, out
):
    rows, lanes = gate.shape
    rest = out.shape[0] - rows

    @pl.when(pick[0] == 0)
    def _():
        out[:rows, :lanes] = gate[...].astype(F32)
        out[:rows, lanes:] = gate_other[...].astype(F32)
        out[rows:, :lanes] = late[:rest, :].astype(F32)
        out[rows:, lanes:] = late_other[:rest, :].astype(F32)

    @pl.when(pick[0] != 0)
    def _():
        out[:rows, :lanes] = second_other[:rows, :].astype(F32)
        out[:rows, lanes:] = second[:rows, :].astype(F32)
        out[rows:, :lanes] = out_and_cd_other[DI:, :].astype(F32)
        out[rows:, lanes:] = out_and_cd[DI:, :].astype(F32)


def place_out_kernel(pick, first, first_other, second, second_other, out):
    lanes = first.shape[1]
    half = out.shape[0] // 2

    def write(at, block, start):
        for column in range(out.shape[1] // lanes):
            out[at : at + half, column * lanes : (column + 1) * lanes] = block[
                start + column * half : start + (column + 1) * half, :
            ].astype(F32)

    @pl.when(pick[0] == 0)
    def _():
        write(0, first, 0)
        write(half, first_other, 0)

    @pl.when(pick[0] != 0)
    def _():
        write(0, second_other, DI)
        write(half, second, DI)


def call(body, outs, scratch, *operands):
    whole = pl.BlockSpec(memory_space=pltpu.VMEM)
    scalars = [pl.BlockSpec(memory_space=pltpu.SMEM)] if operands[0].dtype == jnp.int32 else []
    return pl.pallas_call(
        body,
        out_shape=[jax.ShapeDtypeStruct(shape, kind) for shape, kind in outs],
        in_specs=scalars + [whole] * (len(operands) - len(scalars)),
        out_specs=[whole] * len(outs),
        scratch_shapes=[pltpu.VMEM(shape, kind) for shape, kind in scratch],
        compiler_params=pltpu.CompilerParams(vmem_limit_bytes=56 * 1024 * 1024),
    )(*operands)


def turned(block, axis, distance):
    count = lax.axis_size(axis)
    return lax.ppermute(block, axis, [(i, (i + distance) % count) for i in range(count)])


def from_behind(block, distance):
    count = lax.axis_size("seq")
    route = [(i - distance, i) for i in range(count) if 0 <= i - distance < count]
    return lax.ppermute(block, "seq", route)


def together(*values):
    return lax.optimization_barrier(values)


def neighbours():
    return [(i, i ^ 1) for i in range(lax.axis_size("seq"))]


def exchange_states(message, reverse, beside, then=None):
    count = lax.axis_size("seq")
    rows = N // count
    sent = message.reshape(count, rows, MESSAGE)
    gathered = lax.all_to_all(sent, "seq", 0, 0)
    gathered, beside = together(gathered, beside)

    def body(gathered_ref, out_ref):
        carry_kernel(reverse, gathered_ref, out_ref)

    (states,) = call(body, [((count, rows, DI), message.dtype)], [], gathered)
    if then is not None:
        states = then(states)
    return lax.all_to_all(states, "seq", 0, 0).reshape(N, DI), beside


class SeqSum:
    def __init__(self, part):
        count = lax.axis_size("seq")
        self.parity = lax.axis_index("seq") % 2
        self.others = count // 2
        self.groups = [[2 * i + p for i in range(self.others)] for p in range(2)]
        self.half, self.lanes = part.shape[0] // 2, part.shape[1]
        self.keep = lax.dynamic_slice_in_dim(part, self.parity * self.half, self.half, 0)
        self.sent = lax.dynamic_slice_in_dim(part, (1 - self.parity) * self.half, self.half, 0)

    def move(self):
        self.moving = lax.ppermute(self.sent, "seq", neighbours())
        return self

    def over_others(self, split):
        return lax.all_to_all(split, "seq", 0, 0, axis_index_groups=self.groups)

    def scatter(self):
        both = (self.keep.astype(F32) + self.moving.astype(F32)).astype(BF16)
        self.split = both.reshape(self.others, self.half // self.others, self.lanes)
        self.moving = self.over_others(self.split)

    def gather(self):
        total = jnp.sum(self.moving.astype(F32), axis=0).astype(BF16)
        self.copies = jnp.broadcast_to(total, (self.others,) + total.shape)
        self.moving = self.over_others(self.copies)

    def swap(self):
        self.own = self.moving.reshape(self.half, self.lanes)
        self.moving = lax.ppermute(self.own, "seq", neighbours())

    def whole(self):
        return jnp.where(
            self.parity == 0,
            jnp.concatenate([self.own, self.moving], axis=0),
            jnp.concatenate([self.moving, self.own], axis=0),
        )


def on_device(
    inputs,
    cotangent,
    boundary,
    norm_gain,
    w_in,
    conv_w,
    conv_b,
    dt_bias,
    a_log,
    skip_gain,
    gate_norm,
    w_out,
):
    section = lax.axis_index("section")
    sections = lax.axis_size("section")
    shard = lax.axis_index("wshard")
    shards = lax.axis_size("wshard")
    parity = lax.axis_index("seq") % 2
    batches, _, rows, _ = inputs.shape
    is_first = section == 0

    offset = lax.axis_index("seq") * rows
    source = lax.dynamic_index_in_dim(inputs[:, 0], section, keepdims=False)
    upstream = lax.dynamic_index_in_dim(cotangent[:, 0], section, keepdims=False)
    bound = lax.dynamic_index_in_dim(boundary[:, 0], section, keepdims=False)

    def held_at(away, which):
        return 2 * away + (which + (parity if away else 0)) % 2

    def held_halves():
        out = []
        for away in range(shards):
            for half in range(2):
                which = (half + (parity if away else 0)) % 2
                out.append(2 * ((shard + away) % shards) + which)
        return out

    held = held_halves()

    def to_held(values):
        half = values.shape[1] // (2 * shards)
        own = lax.dynamic_slice_in_dim(values, held[0] * half, 2 * half, 1)
        rest = [lax.dynamic_slice_in_dim(values, at * half, half, 1) for at in held[2:]]
        return jnp.concatenate([own] + rest, axis=1)

    def from_held(values):
        half = values.shape[1] // (2 * shards)
        out = jnp.zeros(values.shape, values.dtype)
        out = lax.dynamic_update_slice_in_dim(out, values[:, : 2 * half], held[0] * half, 1)
        for place_held, at in enumerate(held[2:], 2):
            piece = values[:, place_held * half : (place_held + 1) * half]
            out = lax.dynamic_update_slice_in_dim(out, piece, at * half, 1)
        return out

    half_out = DI // (2 * shards)
    held_starts = []
    for block in range(shards):
        away = (block - shard) % shards
        for which in range(2):
            turn = jnp.where(away == 0, 0, parity)
            held_starts.append((2 * away + (which + turn) % 2) * half_out)
    place = jnp.stack([offset, bound] + held_starts).astype(jnp.int32)

    small_parts = (norm_gain, conv_w, conv_b, dt_bias, a_log, skip_gain, gate_norm)
    flat = jnp.concatenate([part.reshape(-1) for part in small_parts])
    flats = jnp.stack([flat] + [turned(flat, "wshard", -away) for away in range(1, shards)])
    flats = jnp.concatenate([flats, flats], axis=0)
    flats = lax.dynamic_slice_in_dim(flats, (shards - shard) % shards, shards, 0)
    flats_other = turned(flats, "section", 1)

    turned_in = jnp.swapaxes(w_in[0], 0, 1)
    own_pieces = [(turned_in[DI:], 1), (turned_in[:DI], 1), (w_out[0], 0)]
    halves = [
        lax.dynamic_slice_in_dim(own, parity * own.shape[dim] // 2, own.shape[dim] // 2, dim)
        for own, dim in own_pieces
    ]

    def fetch(sent):
        return [turned(sent, "wshard", -away) for away in range(1, shards)]

    def beside(got):
        return [lax.ppermute(block, "seq", neighbours()) for block in got]

    def joined(which, got, other):
        pairs = [block for pair in zip(got, other) for block in pair]
        return lax.all_gather(jnp.concatenate(pairs, axis=own_pieces[which][1]), "section")

    weights = [[lax.all_gather(own, "section"), None] for own, _ in own_pieces]
    got_cd = fetch(halves[0])
    sent_gate, got_cd, flats, flats_other = together(halves[1], got_cd, flats, flats_other)
    got_gate = fetch(sent_gate)
    other_cd = beside(got_cd)
    got_gate, other_cd = lax.optimization_barrier((got_gate, other_cd))
    weights[0][1] = joined(0, got_cd, other_cd)
    other_gate = beside(got_gate)
    sent_out, got_gate = together(halves[2], got_gate)
    got_out = fetch(sent_out)

    def complete_gate(cd):
        cd, got, other = together(cd, got_gate, other_gate)
        weights[1][1] = joined(1, got, other)
        return cd

    def start_out(event):
        got, event = together(got_out, event)
        weights[2][1] = (got, beside(got))
        return event

    def complete_out(event):
        got, other = weights[2][1]
        got, other, event = together(got, other, event)
        weights[2][1] = joined(2, got, other)
        return event

    def split(values):
        cut = values.shape[1] // shards
        return values[:, :cut], values[:, cut:]

    def from_rows(which, layer, values):
        own, rest = weights[which]
        first, second = split(values)
        return dot_nt(first, own[layer]) + dot_nt(second, rest[layer])

    def to_rows(terms, layer):
        own = sum(dot(values, weights[which][0][layer]) for which, values in terms)
        rest = sum(dot(values, weights[which][1][layer]) for which, values in terms)
        return jnp.concatenate([own, rest], axis=1)

    def small_of(layer):
        every = jnp.where(section == layer, flats, flats_other)
        out, at = [], 0
        for part in small_parts:
            size = part.size
            piece = every[:, at : at + size].reshape((shards,) + part.shape[1:])
            at += size
            if part.ndim == 3:
                out.append(jnp.moveaxis(piece, 0, 1).reshape(part.shape[1], -1))
            else:
                out.append(piece.reshape(1, -1))
        return out

    def layer_forward(layer, hidden_low):
        gain_pre, taps, conv_bias, bias_dt, log_rate, skip, gain_gate = small_of(layer)
        hidden = hidden_low.astype(F32)
        scale = lax.rsqrt(jnp.mean(hidden * hidden, axis=-1, keepdims=True) + EPSILON)
        normed_low = to_held((hidden * scale * gain_pre).astype(BF16))
        cd = from_rows(0, layer, normed_low)
        if layer == 0:
            cd = complete_gate(cd)
        edge = from_behind(cd[rows - EDGE :, :DCONV], 1)
        gate = from_rows(1, layer, normed_low)
        pre, act, step, cum, message = call(
            states_kernel,
            [
                ((rows, DCONV), F32),
                ((rows, DCONV), F32),
                ((rows, H), F32),
                ((rows, H), F32),
                ((N, MESSAGE), F32),
            ],
            [],
            place,
            cd,
            edge,
            taps,
            conv_bias,
            bias_dt,
            log_rate,
        )
        if layer == 0:
            message = start_out(message)
        entry, gate = exchange_states(message, False, gate, complete_out if layer == 0 else None)
        (local,) = call(intra_kernel, [((rows, DI), F32)], [], place, act, step, cum, skip)
        mixed, gated_low = call(
            gate_kernel,
            [((rows, DI), F32), ((rows, DI), BF16)],
            [((rows, DI), F32)],
            place,
            entry,
            local,
            act,
            cum,
            gate,
            gain_gate,
        )
        own, rest = weights[2]
        first, second = split(gated_low)
        result = (hidden + dot(first, own[layer]) + dot(second, rest[layer])).astype(BF16)
        kept = (hidden, scale, normed_low, cd, edge, gate, pre, act, step, cum, entry, mixed, gated_low)
        return result, kept

    def columns_for(low, core, away):
        half = low.shape[1] // (2 * shards)
        return lax.dynamic_slice_in_dim(low, held_at(away, core) * half, half, 1)

    class Near:
        def __init__(self, product, low):
            self.product, self.low = product, low
            self.sent = [
                product(columns_for(low, 1 - section, away)).astype(BF16) for away in range(shards)
            ]

        def kept(self, away):
            part = self.product(columns_for(self.low, section, away))
            return part + turned(self.sent[away], "section", 1).astype(F32)

        def add_section(self):
            self.blocks = [self.kept(away).astype(BF16) for away in range(1, shards)]

        def add_shards(self):
            total = self.kept(0)
            for away, block in enumerate(self.blocks, 1):
                total = total + turned(block, "wshard", away).astype(F32)
            return total.astype(BF16)

    def near_in(low, up):
        return Near(lambda columns: dot_tn(up, columns), low)

    def near_out(low, up):
        return Near(lambda columns: dot_tn(columns, up), low)

    lanes = D // (2 * shards)

    def lay_out(total):
        return jnp.concatenate(jnp.split(total, D // lanes, axis=1), axis=0)

    def layer_backward(layer, up_low, kept, beside, before=None, summing=None):
        gain_pre, taps, conv_bias, bias_dt, log_rate, skip, gain_gate = small_of(layer)
        hidden, scale, normed_low, cd, edge, gate, pre, act, step, cum, entry, mixed, gated_low = kept
        near = near_out(gated_low, up_low)
        own, rest = weights[2]
        grad_gated = jnp.concatenate([dot_nt(up_low, own[layer]), dot_nt(up_low, rest[layer])], axis=1)
        grad_gated, near.sent = together(grad_gated, near.sent)
        if before is not None:
            before.add_section()
            grad_gated, before.blocks = together(grad_gated, before.blocks)
        grad_mixed, grad_gate, grad_gain_gate, message = call(
            gate_back_kernel,
            [
                ((rows, DI), F32),
                ((rows, DI), BF16),
                ((1, DI), F32),
                ((N, MESSAGE), BF16),
            ],
            [((rows, DI), F32)],
            place,
            grad_gated,
            mixed,
            gate,
            gain_gate,
            cum,
            act,
        )
        near_gate = near_in(normed_low, grad_gate)
        near.add_section()
        grad_mixed, near_gate.sent, near.blocks = together(grad_mixed, near_gate.sent, near.blocks)
        grad_scaled, grad_bc, grad_cum = call(
            intra_back_kernel,
            [((rows, DI), F32), ((rows, 2 * N), F32), ((rows, H), F32)],
            [((rows, rows), F32), ((H, rows), F32)],
            place,
            act,
            step,
            cum,
            grad_mixed,
            entry,
        )
        held_back = () if summing is None else summing.moving
        leaving, (grad_scaled, held_back) = exchange_states(message, True, (grad_scaled, held_back))
        if summing is not None:
            summing.moving = held_back
            summing.scatter()
            grad_scaled, summing.split = together(grad_scaled, summing.split)
        near_gate.add_section()
        grad_scaled, near_gate.blocks, beside = together(grad_scaled, near_gate.blocks, beside)
        grad_cd, grad_tail, grad_edge, grad_taps, grad_conv_bias, grad_heads = call(
            finish_kernel,
            [
                ((rows, DCD), BF16),
                ((EDGE, DCONV), F32),
                ((EDGE, DCONV), F32),
                ((K, DCONV), F32),
                ((1, DCONV), F32),
                ((EDGE, H), F32),
            ],
            [((rows, DCONV), F32)],
            place,
            cd,
            edge,
            pre,
            act,
            step,
            cum,
            grad_mixed,
            grad_scaled,
            grad_bc,
            grad_cum,
            entry,
            leaving,
            taps,
            bias_dt,
            log_rate,
            skip,
        )
        edge_back = from_behind(grad_edge, -1)
        sum_out = lay_out(near.add_shards())
        if before is not None:
            sum_out = SeqSum(jnp.concatenate([sum_out, before.add_shards()], axis=0))
            summing.gather()
            edge_back, sum_out.sent, summing.copies = together(
                edge_back, sum_out.sent, summing.copies
            )
            sum_out.move()
        else:
            edge_back, sum_out = together(edge_back, sum_out)
        part_gate = near_gate.add_shards()
        edge_back, part_gate = together(edge_back, part_gate)
        grad_cd = lax.dynamic_update_slice(
            grad_cd, (grad_tail + edge_back).astype(BF16), (rows - EDGE, 0)
        )
        grad_normed = from_held(to_rows([(0, grad_cd), (1, grad_gate)], layer))
        grad_pulled = grad_normed * gain_pre
        cross = jnp.mean(grad_pulled * hidden, axis=-1, keepdims=True)
        grad_hidden = up_low.astype(F32) + scale * grad_pulled - scale**3 * cross * hidden
        grad_gain_pre = jnp.sum(grad_normed * hidden * scale, axis=0)
        small = (
            grad_gain_pre,
            grad_taps,
            grad_conv_bias,
            grad_heads[0],
            grad_heads[1],
            grad_heads[2],
            grad_gain_gate,
        )
        return grad_hidden, (sum_out, part_gate, grad_cd), small, beside

    middle, kept_first = layer_forward(0, source)
    ending, kept_second = layer_forward(1, middle)
    def placed(first, second):
        own = jnp.where(is_first, first, second)
        other = turned(jnp.where(is_first, second, first), "section", 1).astype(own.dtype)
        both = jnp.stack([jnp.where(is_first, own, other), jnp.where(is_first, other, own)])
        return both.reshape(1, batches, 1, rows, D)

    def placed_grads(first, second_low):
        own = jnp.where(is_first, first, second_low.astype(F32))
        sent = jnp.where(is_first, second_low, first.astype(BF16))
        other = turned(sent, "section", 1).astype(F32)
        both = jnp.stack([jnp.where(is_first, own, other), jnp.where(is_first, other, own)])
        return both.reshape(1, batches, 1, rows, D)

    grad_middle, (out_second, gate_second, grad_cd), small_second, acts = layer_backward(
        1, upstream, kept_second, placed(middle, ending)
    )
    grad_middle_low = grad_middle.astype(BF16)
    sums_second = jnp.concatenate([gate_second, out_second], axis=0)
    cd_second = near_in(kept_second[2], grad_cd)
    sums_second, grad_middle_low, cd_second.sent = together(
        sums_second, grad_middle_low, cd_second.sent
    )
    sums_second = SeqSum(sums_second).move()
    grad_source, (sums_out, gate_first, grad_cd), small_first, _ = layer_backward(
        0, grad_middle_low, kept_first, (), cd_second, sums_second
    )
    extra_rows = -(-sum(part.size for part in small_first) // (8 * 16 * lanes)) * 8 * 16

    def small_block(small):
        flat_grads = jnp.concatenate([part.reshape(-1) for part in small])
        flat_grads = jnp.pad(flat_grads, (0, extra_rows * lanes - flat_grads.size))
        return flat_grads.reshape(extra_rows, lanes)

    block_first, block_second = small_block(small_first), small_block(small_second)
    extra = jnp.where(is_first, block_first, block_second)
    extra_sent = jnp.where(is_first, block_second, block_first).astype(BF16)

    cd_first = near_in(kept_first[2], grad_cd)
    extra = extra + turned(extra_sent, "section", 1).astype(F32)
    sums_gate = SeqSum(gate_first).move()
    sums_out.scatter()
    cd_first.sent, sums_out.split = together(cd_first.sent, sums_out.split)
    sums_second.swap()
    cd_first.add_section()
    cd_first.blocks = [
        jnp.concatenate([block, extra.astype(BF16)], axis=0) for block in cd_first.blocks
    ]
    sums_second.own, cd_first.blocks = together(sums_second.own, cd_first.blocks)
    got_blocks = [turned(block, "wshard", away) for away, block in enumerate(cd_first.blocks, 1)]
    late = jnp.concatenate([cd_first.kept(0), extra], axis=0)
    late = (late + sum(block.astype(F32) for block in got_blocks)).astype(BF16)
    sums_gate.scatter()
    second = sums_second.whole()
    late, second, sums_gate.split = together(late, second, sums_gate.split)
    late = SeqSum(late).move()
    sums_out.gather()
    late.moving, sums_out.copies = together(late.moving, sums_out.copies)
    late.scatter()
    in_grad = placed_grads(grad_source, grad_middle_low)
    sums_out.swap()
    sums_out.own, late.split, in_grad = together(sums_out.own, late.split, in_grad)
    sums_gate.gather()
    late.gather()
    late.copies, sums_gate.copies = together(late.copies, sums_gate.copies)
    out_and_cd = sums_out.whole()
    sums_gate.swap()
    pick = section.astype(jnp.int32).reshape(1)

    def crossed(block, route):
        return [block, lax.ppermute(block, "section", route)]

    known = crossed(out_and_cd, [(0, 1), (1, 0)]) + crossed(second, [(0, 1)])
    (part_out,) = call(place_out_kernel, [((DI // shards, D), F32)], [], pick, *known)
    late.moving, part_out, known = together(late.moving, part_out, known)
    late.swap()
    gate_first, late_first = sums_gate.whole(), late.whole()
    (part_in,) = call(
        place_kernel,
        [((DI + DCD, 2 * lanes), F32)],
        [],
        pick,
        *crossed(gate_first, [(1, 0)]),
        *crossed(late_first, [(1, 0)]),
        *known,
    )
    mine = late_first[DCD:].astype(F32).reshape(-1)
    small_out, at = [], 0
    for part, shown in zip(small_first, small_parts):
        piece = mine[at : at + part.size].reshape(part.shape)
        at += part.size
        width = shown.shape[-1]
        piece = lax.dynamic_slice_in_dim(piece, shard * width, width, piece.ndim - 1)
        small_out.append(piece.reshape(shown.shape))
    return (
        acts,
        in_grad,
        small_out[0],
        jnp.swapaxes(part_in, 0, 1)[None],
        *small_out[1:],
        part_out[None],
    )


def solution(mesh):
    placed = (
        P(None, "wshard", "seq", None),
        P(None, "wshard", "seq", None),
        P(None, "wshard"),
        P("section", "wshard"),
        P("section", "wshard", None),
        P("section", None, "wshard"),
        P("section", "wshard"),
        P("section", "wshard"),
        P("section", "wshard"),
        P("section", "wshard"),
        P("section", "wshard"),
        P("section", "wshard", None),
    )
    return jax.shard_map(
        on_device,
        mesh=mesh,
        in_specs=placed,
        out_specs=(
            P("section", None, "wshard", "seq", None),
            P("section", None, "wshard", "seq", None),
            P("section", "wshard"),
            P("section", "wshard", None),
            P("section", None, "wshard"),
            P("section", "wshard"),
            P("section", "wshard"),
            P("section", "wshard"),
            P("section", "wshard"),
            P("section", "wshard"),
            P("section", "wshard", None),
        ),
        check_vma=False,
    )
```

```python
import jax
import jax.numpy as jnp
from jax import lax
from jax.experimental import pallas as pl
from jax.experimental.pallas import tpu as pltpu
from jax.sharding import PartitionSpec as P

D = 1024
DI = 2048
H = 32
HEAD = DI // H
N = 128
K = 4
DCONV = 2304
DCD = DCONV + H
PAIR = 2 * HEAD
WIDE = 512
BLOCK = 256
EDGE = 8
MESSAGE = DI + 128
EPSILON = 1e-05
LOG2E = 1.4426950408889634
FAR = -1e30
F32 = jnp.float32
BF16 = jnp.bfloat16
HIGH = lax.Precision.HIGHEST


def dot(a, b):
    return jnp.dot(a, b, preferred_element_type=F32)


def dot_nt(a, b):
    return lax.dot_general(a, b, (((1,), (1,)), ((), ())), preferred_element_type=F32)


def dot_tn(a, b):
    return lax.dot_general(a, b, (((0,), (0,)), ((), ())), preferred_element_type=F32)


def iota(shape, dim):
    return lax.broadcasted_iota(jnp.int32, shape, dim)


def ones_where(condition):
    return jnp.where(condition, 1.0, 0.0).astype(F32)


def two_parts(values):
    high = values.astype(BF16)
    return high, (values - high.astype(F32)).astype(BF16)


def spread(values, start, width):
    pick = ones_where((start + iota((H, width), 1)) // HEAD == iota((H, width), 0)).astype(BF16)
    high, low = two_parts(values)
    return dot(high, pick) + dot(low, pick)


def head_sums(values, start):
    width = values.shape[1]
    pick = ones_where((start + iota((width, H), 0)) // HEAD == iota((width, H), 1)).astype(BF16)
    high, low = two_parts(values)
    return dot(high, pick) + dot(low, pick)


def sigmoid(values):
    return 0.5 * jnp.tanh(0.5 * values) + 0.5


def rows_of_one(row):
    return jnp.broadcast_to(row, (EDGE, row.shape[1]))


def segments(place, rows):
    offset, bound = place[0], place[1]
    position = offset + iota((rows, 1), 0)
    segment = ones_where(position >= bound)
    before = jnp.where(offset - 1 >= bound, 1.0, 0.0).astype(F32)
    last = jnp.where(offset + rows - 1 >= bound, 1.0, 0.0).astype(F32)
    return position, segment, before, last


def tap_masks(place, position):
    bound = place[1]
    return [
        ones_where((position - back >= bound) == (position >= bound)) if back else None
        for back in range(K)
    ]


def decay_lanes(through):
    high, low = two_parts(jnp.broadcast_to(through, (N, H)))
    first = ones_where(iota((H, 128), 0) == iota((H, 128), 1)).astype(BF16)
    second = ones_where(iota((H, 128), 0) + H == iota((H, 128), 1)).astype(BF16)
    return dot(high, first) + dot(low, second)


def states_kernel(place, cd, edge, conv_w, conv_b, dt_bias, a_log, pre, act, step, cum, message):
    rows = cd.shape[0]
    position, segment, before, last = segments(place, rows)
    masks = tap_masks(place, position)
    step_now = jax.nn.softplus(cd[:, DCONV:] + dt_bias[...])
    log_decay = -step_now * jnp.exp(a_log[...])
    lower = ones_where(iota((rows, rows), 0) >= iota((rows, rows), 1))
    summed = jnp.dot(lower, log_decay, precision=HIGH, preferred_element_type=F32)
    step[...] = step_now
    cum[...] = summed
    total = summed[rows - 1 :, :]
    weight = step_now * jnp.where(segment == last, jnp.exp(total - summed), 0.0)
    for start in range(0, DCONV, BLOCK):
        here = slice(start, start + BLOCK)
        values = cd[:, here]
        extended = jnp.concatenate([edge[:, here], values], axis=0)
        conv = conv_b[:, here] + conv_w[K - 1 : K, here] * values
        for back in range(1, K):
            moved = pltpu.roll(extended, back, 0)[EDGE:]
            conv = conv + conv_w[K - 1 - back : K - back, here] * moved * masks[back]
        pre[:, here] = conv
        act[:, here] = conv * sigmoid(conv)
    in_high, in_low = two_parts(jnp.transpose(act[:, DI : DI + N]))
    for start in range(0, DI, WIDE):
        here = slice(start, start + WIDE)
        high, low = two_parts(act[:, here] * spread(weight, start, WIDE))
        message[:, here] = dot(in_high, high) + dot(in_high, low) + dot(in_low, high)
    through = jnp.exp(total) * jnp.where(before == last, 1.0, 0.0)
    message[:, DI:] = decay_lanes(through).astype(message.dtype)


def carry_kernel(reverse, gathered, out, *scratch):
    count, rows = gathered.shape[0], gathered.shape[1]
    pick = ones_where(iota((2 * H, DI), 1) // HEAD == iota((2 * H, DI), 0) % H).astype(BF16)
    state = jnp.zeros((rows, DI), F32)
    for source in range(count - 1, -1, -1) if reverse else range(count):
        out[source] = state.astype(out.dtype)
        part = gathered[source]
        through = dot(part[:, DI : DI + 2 * H].astype(BF16), pick)
        state = through * state + part[:, :DI].astype(F32)


def intra_kernel(place, act, step, cum, skip, local):
    rows = act.shape[0]
    position, segment, _, _ = segments(place, rows)
    scores = lax.dot_general(
        act[:, DI + N :],
        act[:, DI : DI + N],
        (((1,), (1,)), ((), ())),
        precision=HIGH,
        preferred_element_type=F32,
    )
    across = place[0] + iota((1, rows), 1)
    same = segment == ones_where(across >= place[1])
    bias = jnp.where((position >= across) & same, 0.0, FAR)
    level = cum[...] * LOG2E
    level_t = jnp.transpose(level)
    steps = step[...]
    skips = rows_of_one(skip[...])
    left = iota((rows, PAIR), 1) < HEAD
    for pair in range(H // 2):
        start = pair * PAIR
        here = slice(start, start + PAIR)
        values = act[:, here]
        high, low = two_parts(values * spread(steps, start, PAIR))
        scaled = jnp.concatenate([high, low], axis=1)
        outs = []
        for head in (2 * pair, 2 * pair + 1):
            decay = jnp.exp2(level[:, head : head + 1] - level_t[head : head + 1, :] + bias)
            first, second = two_parts(decay * scores)
            both = dot(first, scaled)
            outs.append(both[:, :PAIR] + both[:, PAIR:] + dot(second, high))
        local[:, here] = jnp.where(left, outs[0], outs[1]) + spread(skips, start, PAIR)[:1] * values


def gate_kernel(place, entry, local, act, cum, gate, gain, mixed, gated, kept):
    rows = act.shape[0]
    _, segment, before, _ = segments(place, rows)
    enter = jnp.exp(cum[...]) * ones_where(segment == before)
    out_high, out_low = two_parts(act[:, DI + N :])
    square = jnp.zeros((rows, 1), F32)
    for start in range(0, DI, WIDE):
        here = slice(start, start + WIDE)
        high, low = two_parts(entry[:, here])
        entered = dot(out_high, high) + dot(out_low, high) + dot(out_high, low)
        y = local[:, here] + entered * spread(enter, start, WIDE)
        mixed[:, here] = y
        raw = gate[:, here]
        u = y * raw * sigmoid(raw)
        kept[:, here] = u
        square = square + jnp.sum(u * u, axis=1, keepdims=True)
    scale = lax.rsqrt(square / DI + EPSILON)
    count = place.shape[0] - 2
    width = DI // count
    for group in range(count):
        here = slice(group * width, (group + 1) * width)
        there = pl.ds(pl.multiple_of(place[2 + group], 128), width)
        gated[:, there] = (kept[:, here] * scale * gain[:, here]).astype(BF16)


def gate_back_kernel(
    place, grad_gated, mixed, gate, gain, cum, act, grad_mixed, grad_gate, grad_gain, message, kept
):
    rows = act.shape[0]
    _, segment, before, last = segments(place, rows)
    summed = cum[...]
    enter = jnp.exp(summed) * ones_where(segment == before)
    out_t = jnp.transpose(act[:, DI + N :]).astype(BF16)
    square = jnp.zeros((rows, 1), F32)
    cross = jnp.zeros((rows, 1), F32)
    count = place.shape[0] - 2
    width = DI // count
    for group in range(count):
        here = slice(group * width, (group + 1) * width)
        there = pl.ds(pl.multiple_of(place[2 + group], 128), width)
        raw = gate[:, here]
        u = mixed[:, here] * raw * sigmoid(raw)
        kept[:, here] = u
        square = square + jnp.sum(u * u, axis=1, keepdims=True)
        cross = cross + jnp.sum(grad_gated[:, there] * gain[:, here] * u, axis=1, keepdims=True)
    scale = lax.rsqrt(square / DI + EPSILON)
    pulled = scale * scale * scale * cross / DI
    for group in range(count):
        start = group * width
        here = slice(start, start + width)
        there = pl.ds(pl.multiple_of(place[2 + group], 128), width)
        raw = gate[:, here]
        u = kept[:, here]
        up = grad_gated[:, there]
        grad_gain[:, here] = jnp.sum(up * u * scale, axis=0, keepdims=True)
        grad_u = scale * up * gain[:, here] - pulled * u
        curve = sigmoid(raw)
        grad_y = grad_u * raw * curve
        grad_gate[:, here] = (
            grad_u * mixed[:, here] * curve * (1.0 + raw * (1.0 - curve))
        ).astype(BF16)
        grad_mixed[:, here] = grad_y
        pull = (grad_y * spread(enter, start, width)).astype(BF16)
        message[:, here] = dot(out_t, pull).astype(BF16)
    through = jnp.exp(summed[rows - 1 :, :]) * jnp.where(before == last, 1.0, 0.0)
    message[:, DI:] = decay_lanes(through).astype(message.dtype)


def intra_back_kernel(
    place, act, step, cum, grad_mixed, entry, grad_scaled, grad_bc, grad_cum, grad_scores, across_sum
):
    rows = act.shape[0]
    position, segment, before, _ = segments(place, rows)
    in_b = act[:, DI : DI + N].astype(BF16)
    out_c = act[:, DI + N :].astype(BF16)
    scores = dot_nt(in_b, out_c)
    across = place[0] + iota((1, rows), 1)
    same = segment == ones_where(across >= place[1])
    bias = jnp.where((across >= position) & same, 0.0, FAR)
    summed = cum[...]
    level = summed * LOG2E
    level_t = jnp.transpose(level)
    steps = step[...]
    left = iota((rows, PAIR), 1) < HEAD
    lane = iota((rows, H), 1)
    grad_scores[...] = jnp.zeros((rows, rows), F32)
    down_sum = jnp.zeros((rows, H), F32)
    for pair in range(H // 2):
        start = pair * PAIR
        here = slice(start, start + PAIR)
        scaled = act[:, here] * spread(steps, start, PAIR)
        up = grad_mixed[:, here].astype(BF16)
        outs = []
        for head in (2 * pair, 2 * pair + 1):
            mine = left if head % 2 == 0 else jnp.logical_not(left)
            grad_weight = dot_nt(jnp.where(mine, scaled, 0.0).astype(BF16), up)
            decay = jnp.exp2(level_t[head : head + 1, :] - level[:, head : head + 1] + bias)
            weight = decay * scores
            grad_scores[...] += decay * grad_weight
            flow = weight * grad_weight
            across_sum[head : head + 1, :] = jnp.sum(flow, axis=0, keepdims=True)
            down_sum = down_sum + jnp.where(lane == head, jnp.sum(flow, axis=1, keepdims=True), 0.0)
            outs.append(dot(weight.astype(BF16), up))
        grad_scaled[:, here] = jnp.where(left, outs[0], outs[1])
    enter = jnp.exp(summed) * ones_where(segment == before)
    grad_out = jnp.zeros((rows, N), F32)
    grad_enter = jnp.zeros((rows, H), F32)
    for start in range(0, DI, WIDE):
        here = slice(start, start + WIDE)
        entered = entry[:, here].astype(BF16)
        pull = grad_mixed[:, here] * spread(enter, start, WIDE)
        grad_out = grad_out + dot_nt(pull.astype(BF16), entered)
        grad_enter = grad_enter + head_sums(pull * dot(out_c, entered), start)
    low = grad_scores[...].astype(BF16)
    grad_bc[:, :N] = dot(low, out_c)
    grad_bc[:, N:] = grad_out + dot(jnp.transpose(grad_scores[...]).astype(BF16), in_b)
    grad_cum[...] = jnp.transpose(across_sum[...]) - down_sum + grad_enter


def finish_kernel(
    place,
    cd,
    edge,
    pre,
    act,
    step,
    cum,
    grad_mixed,
    grad_scaled,
    grad_bc,
    grad_cum,
    entry,
    leaving,
    conv_w,
    dt_bias,
    a_log,
    skip,
    grad_cd,
    grad_tail,
    grad_edge,
    grad_conv_w,
    grad_conv_b,
    grad_heads,
    grad_pre,
):
    rows = cd.shape[0]
    position, segment, before, last = segments(place, rows)
    masks = tap_masks(place, position)
    summed = cum[...]
    total = summed[rows - 1 :, :]
    to_end = jnp.where(segment == last, jnp.exp(total - summed), 0.0)
    steps = step[...]
    skips = rows_of_one(skip[...])
    in_b = act[:, DI : DI + N].astype(BF16)

    def silu_slope(values):
        curve = sigmoid(values)
        return curve * (1.0 + values * (1.0 - curve))

    grad_end = jnp.zeros((rows, H), F32)
    grad_step = jnp.zeros((rows, H), F32)
    grad_in = grad_bc[:, :N]
    grad_through = jnp.zeros((EDGE, H), F32)
    grad_skip = jnp.zeros((EDGE, H), F32)
    for start in range(0, DI, WIDE):
        here = slice(start, start + WIDE)
        values = act[:, here]
        up = grad_mixed[:, here]
        left = leaving[:, here]
        step_wide = spread(steps, start, WIDE)
        end_wide = spread(to_end, start, WIDE)
        pulled = dot(in_b, left) * end_wide
        scaled = values * step_wide
        grad_now = grad_scaled[:, here] + pulled
        grad_end = grad_end + head_sums(scaled * pulled, start)
        grad_step = grad_step + head_sums(grad_now * values, start)
        grad_in = grad_in + dot_nt((end_wide * scaled).astype(BF16), left)
        states = jnp.sum(entry[:, here].astype(F32) * left.astype(F32), axis=0, keepdims=True)
        grad_through = grad_through + head_sums(rows_of_one(states), start)
        skipped = jnp.sum(up * values, axis=0, keepdims=True)
        grad_skip = grad_skip + head_sums(rows_of_one(skipped), start)
        grad_x = grad_now * step_wide + spread(skips, start, WIDE)[:1] * up
        grad_pre[:, here] = grad_x * silu_slope(pre[:, here])
    grad_pre[:, DI : DI + N] = grad_in * silu_slope(pre[:, DI : DI + N])
    grad_pre[:, DI + N :] = grad_bc[:, N:] * silu_slope(pre[:, DI + N :])
    through = jnp.exp(total) * jnp.where(before == last, 1.0, 0.0)
    at_last = jnp.sum(grad_end, axis=0, keepdims=True) + through * grad_through[:1]
    upper = ones_where(iota((rows, rows), 1) >= iota((rows, rows), 0))
    grad_log = at_last + jnp.dot(
        upper, grad_cum[...] - grad_end, precision=HIGH, preferred_element_type=F32
    )
    rate = jnp.exp(a_log[...])
    grad_step = grad_step - rate * grad_log
    grad_raw = grad_step * sigmoid(cd[:, DCONV:] + dt_bias[...])
    grad_cd[:, DCONV:] = grad_raw.astype(BF16)
    grad_heads[0:1, :] = jnp.sum(grad_raw, axis=0, keepdims=True)
    grad_heads[1:2, :] = jnp.sum(grad_log * -steps * rate, axis=0, keepdims=True)
    grad_heads[2:3, :] = grad_skip[:1]
    grad_heads[3:, :] = jnp.zeros((EDGE - 3, H), F32)
    nothing = jnp.zeros((EDGE, BLOCK), F32)
    for start in range(0, DCONV, BLOCK):
        here = slice(start, start + BLOCK)
        values = cd[:, here]
        extended = jnp.concatenate([edge[:, here], values], axis=0)
        up = grad_pre[:, here]
        grad_conv_b[:, here] = jnp.sum(up, axis=0, keepdims=True)
        grad_conv_w[K - 1 : K, here] = jnp.sum(up * values, axis=0, keepdims=True)
        spilled = nothing
        grad_in_now = conv_w[K - 1 : K, here] * up
        for back in range(1, K):
            moved = pltpu.roll(extended, back, 0)[EDGE:]
            masked = up * masks[back]
            grad_conv_w[K - 1 - back : K - back, here] = jnp.sum(
                masked * moved, axis=0, keepdims=True
            )
            framed = jnp.concatenate([nothing, masked, nothing], axis=0)
            returned = pltpu.roll(framed, rows + 2 * EDGE - back, 0)
            tap = conv_w[K - 1 - back : K - back, here]
            spilled = spilled + tap * returned[:EDGE]
            grad_in_now = grad_in_now + tap * returned[EDGE : EDGE + rows]
        grad_edge[:, here] = spilled
        grad_tail[:, here] = grad_in_now[rows - EDGE :]
        grad_cd[:, here] = grad_in_now.astype(BF16)


def place_kernel(
    pick, gate, gate_other, late, late_other, out_and_cd, out_and_cd_other, second, second_other, out
):
    rows, lanes = gate.shape
    rest = out.shape[0] - rows

    @pl.when(pick[0] == 0)
    def _():
        out[:rows, :lanes] = gate[...].astype(F32)
        out[:rows, lanes:] = gate_other[...].astype(F32)
        out[rows:, :lanes] = late[:rest, :].astype(F32)
        out[rows:, lanes:] = late_other[:rest, :].astype(F32)

    @pl.when(pick[0] != 0)
    def _():
        out[:rows, :lanes] = second_other[:rows, :].astype(F32)
        out[:rows, lanes:] = second[:rows, :].astype(F32)
        out[rows:, :lanes] = out_and_cd_other[DI:, :].astype(F32)
        out[rows:, lanes:] = out_and_cd[DI:, :].astype(F32)


def place_out_kernel(pick, first, first_other, second, second_other, out):
    lanes = first.shape[1]
    half = out.shape[0] // 2

    def write(at, block, start):
        for column in range(out.shape[1] // lanes):
            out[at : at + half, column * lanes : (column + 1) * lanes] = block[
                start + column * half : start + (column + 1) * half, :
            ].astype(F32)

    @pl.when(pick[0] == 0)
    def _():
        write(0, first, 0)
        write(half, first_other, 0)

    @pl.when(pick[0] != 0)
    def _():
        write(0, second_other, DI)
        write(half, second, DI)


def call(body, outs, scratch, *operands):
    whole = pl.BlockSpec(memory_space=pltpu.VMEM)
    scalars = [pl.BlockSpec(memory_space=pltpu.SMEM)] if operands[0].dtype == jnp.int32 else []
    return pl.pallas_call(
        body,
        out_shape=[jax.ShapeDtypeStruct(shape, kind) for shape, kind in outs],
        in_specs=scalars + [whole] * (len(operands) - len(scalars)),
        out_specs=[whole] * len(outs),
        scratch_shapes=[pltpu.VMEM(shape, kind) for shape, kind in scratch],
        compiler_params=pltpu.CompilerParams(vmem_limit_bytes=56 * 1024 * 1024),
    )(*operands)


def turned(block, axis, distance):
    count = lax.axis_size(axis)
    return lax.ppermute(block, axis, [(i, (i + distance) % count) for i in range(count)])


def from_behind(block, distance):
    count = lax.axis_size("seq")
    route = [(i - distance, i) for i in range(count) if 0 <= i - distance < count]
    return lax.ppermute(block, "seq", route)


def together(*values):
    return lax.optimization_barrier(values)


def neighbours():
    return [(i, i ^ 1) for i in range(lax.axis_size("seq"))]


def exchange_states(message, reverse, beside, then=None):
    count = lax.axis_size("seq")
    rows = N // count
    sent = message.reshape(count, rows, MESSAGE)
    gathered = lax.all_to_all(sent, "seq", 0, 0)
    gathered, beside = together(gathered, beside)

    def body(gathered_ref, out_ref):
        carry_kernel(reverse, gathered_ref, out_ref)

    (states,) = call(body, [((count, rows, DI), message.dtype)], [], gathered)
    if then is not None:
        states = then(states)
    return lax.all_to_all(states, "seq", 0, 0).reshape(N, DI), beside


class SeqSum:
    def __init__(self, part):
        count = lax.axis_size("seq")
        self.parity = lax.axis_index("seq") % 2
        self.others = count // 2
        self.groups = [[2 * i + p for i in range(self.others)] for p in range(2)]
        self.half, self.lanes = part.shape[0] // 2, part.shape[1]
        self.keep = lax.dynamic_slice_in_dim(part, self.parity * self.half, self.half, 0)
        self.sent = lax.dynamic_slice_in_dim(part, (1 - self.parity) * self.half, self.half, 0)

    def move(self):
        self.moving = lax.ppermute(self.sent, "seq", neighbours())
        return self

    def over_others(self, split):
        return lax.all_to_all(split, "seq", 0, 0, axis_index_groups=self.groups)

    def scatter(self):
        both = (self.keep.astype(F32) + self.moving.astype(F32)).astype(BF16)
        self.split = both.reshape(self.others, self.half // self.others, self.lanes)
        self.moving = self.over_others(self.split)

    def gather(self):
        total = jnp.sum(self.moving.astype(F32), axis=0).astype(BF16)
        self.copies = jnp.broadcast_to(total, (self.others,) + total.shape)
        self.moving = self.over_others(self.copies)

    def swap(self):
        self.own = self.moving.reshape(self.half, self.lanes)
        self.moving = lax.ppermute(self.own, "seq", neighbours())

    def whole(self):
        return jnp.where(
            self.parity == 0,
            jnp.concatenate([self.own, self.moving], axis=0),
            jnp.concatenate([self.moving, self.own], axis=0),
        )


def on_device(
    inputs,
    cotangent,
    boundary,
    norm_gain,
    w_in,
    conv_w,
    conv_b,
    dt_bias,
    a_log,
    skip_gain,
    gate_norm,
    w_out,
):
    section = lax.axis_index("section")
    sections = lax.axis_size("section")
    shard = lax.axis_index("wshard")
    shards = lax.axis_size("wshard")
    parity = lax.axis_index("seq") % 2
    batches, _, rows, _ = inputs.shape
    is_first = section == 0

    offset = lax.axis_index("seq") * rows
    source = lax.dynamic_index_in_dim(inputs[:, 0], section, keepdims=False)
    upstream = lax.dynamic_index_in_dim(cotangent[:, 0], section, keepdims=False)
    bound = lax.dynamic_index_in_dim(boundary[:, 0], section, keepdims=False)

    def held_at(away, which):
        return 2 * away + (which + (parity if away else 0)) % 2

    def held_halves():
        out = []
        for away in range(shards):
            for half in range(2):
                which = (half + (parity if away else 0)) % 2
                out.append(2 * ((shard + away) % shards) + which)
        return out

    held = held_halves()

    def to_held(values):
        half = values.shape[1] // (2 * shards)
        own = lax.dynamic_slice_in_dim(values, held[0] * half, 2 * half, 1)
        rest = [lax.dynamic_slice_in_dim(values, at * half, half, 1) for at in held[2:]]
        return jnp.concatenate([own] + rest, axis=1)

    def from_held(values):
        half = values.shape[1] // (2 * shards)
        out = jnp.zeros(values.shape, values.dtype)
        out = lax.dynamic_update_slice_in_dim(out, values[:, : 2 * half], held[0] * half, 1)
        for place_held, at in enumerate(held[2:], 2):
            piece = values[:, place_held * half : (place_held + 1) * half]
            out = lax.dynamic_update_slice_in_dim(out, piece, at * half, 1)
        return out

    half_out = DI // (2 * shards)
    held_starts = []
    for block in range(shards):
        away = (block - shard) % shards
        for which in range(2):
            turn = jnp.where(away == 0, 0, parity)
            held_starts.append((2 * away + (which + turn) % 2) * half_out)
    place = jnp.stack([offset, bound] + held_starts).astype(jnp.int32)

    small_parts = (norm_gain, conv_w, conv_b, dt_bias, a_log, skip_gain, gate_norm)
    flat = jnp.concatenate([part.reshape(-1) for part in small_parts])
    flats = jnp.stack([flat] + [turned(flat, "wshard", -away) for away in range(1, shards)])
    flats = jnp.concatenate([flats, flats], axis=0)
    flats = lax.dynamic_slice_in_dim(flats, (shards - shard) % shards, shards, 0)
    flats_other = turned(flats, "section", 1)

    turned_in = jnp.swapaxes(w_in[0], 0, 1)
    own_pieces = [(turned_in[DI:], 1), (turned_in[:DI], 1), (w_out[0], 0)]
    halves = [
        lax.dynamic_slice_in_dim(own, parity * own.shape[dim] // 2, own.shape[dim] // 2, dim)
        for own, dim in own_pieces
    ]

    def fetch(sent):
        return [turned(sent, "wshard", -away) for away in range(1, shards)]

    def beside(got):
        return [lax.ppermute(block, "seq", neighbours()) for block in got]

    def joined(which, got, other):
        pairs = [block for pair in zip(got, other) for block in pair]
        return lax.all_gather(jnp.concatenate(pairs, axis=own_pieces[which][1]), "section")

    weights = [[lax.all_gather(own, "section"), None] for own, _ in own_pieces]
    cut = DCD // 2
    got_cd = fetch(halves[0][:cut])
    sent_cd, got_cd = together(halves[0][cut:], got_cd)
    got_cd_rest = fetch(sent_cd)
    other_cd = beside(got_cd)
    sent_gate, got_cd_rest, other_cd, flats, flats_other = together(
        halves[1], got_cd_rest, other_cd, flats, flats_other
    )
    got_gate = fetch(sent_gate)
    other_cd_rest = beside(got_cd_rest)
    other_cd, other_cd_rest = together(other_cd, other_cd_rest)

    def stacked(first, second):
        return [jnp.concatenate([a, b], axis=0) for a, b in zip(first, second)]

    got_cd, other_cd = stacked(got_cd, got_cd_rest), stacked(other_cd, other_cd_rest)
    got_gate, other_cd = lax.optimization_barrier((got_gate, other_cd))
    weights[0][1] = joined(0, got_cd, other_cd)
    other_gate = beside(got_gate)
    sent_out, got_gate = together(halves[2], got_gate)
    got_out = fetch(sent_out)

    def complete_gate(cd):
        cd, got, other = together(cd, got_gate, other_gate)
        weights[1][1] = joined(1, got, other)
        return cd

    def start_out(event):
        got, event = together(got_out, event)
        weights[2][1] = (got, beside(got))
        return event

    def complete_out(event):
        got, other = weights[2][1]
        got, other, event = together(got, other, event)
        weights[2][1] = joined(2, got, other)
        return event

    def split(values):
        cut = values.shape[1] // shards
        return values[:, :cut], values[:, cut:]

    def from_rows(which, layer, values):
        own, rest = weights[which]
        first, second = split(values)
        return dot_nt(first, own[layer]) + dot_nt(second, rest[layer])

    def to_rows(terms, layer):
        own = sum(dot(values, weights[which][0][layer]) for which, values in terms)
        rest = sum(dot(values, weights[which][1][layer]) for which, values in terms)
        return jnp.concatenate([own, rest], axis=1)

    def small_of(layer):
        every = jnp.where(section == layer, flats, flats_other)
        out, at = [], 0
        for part in small_parts:
            size = part.size
            piece = every[:, at : at + size].reshape((shards,) + part.shape[1:])
            at += size
            if part.ndim == 3:
                out.append(jnp.moveaxis(piece, 0, 1).reshape(part.shape[1], -1))
            else:
                out.append(piece.reshape(1, -1))
        return out

    def layer_forward(layer, hidden_low):
        gain_pre, taps, conv_bias, bias_dt, log_rate, skip, gain_gate = small_of(layer)
        hidden = hidden_low.astype(F32)
        scale = lax.rsqrt(jnp.mean(hidden * hidden, axis=-1, keepdims=True) + EPSILON)
        normed_low = to_held((hidden * scale * gain_pre).astype(BF16))
        cd = from_rows(0, layer, normed_low)
        if layer == 0:
            cd = complete_gate(cd)
        edge = from_behind(cd[rows - EDGE :, :DCONV], 1)
        gate = from_rows(1, layer, normed_low)
        pre, act, step, cum, message = call(
            states_kernel,
            [
                ((rows, DCONV), F32),
                ((rows, DCONV), F32),
                ((rows, H), F32),
                ((rows, H), F32),
                ((N, MESSAGE), F32),
            ],
            [],
            place,
            cd,
            edge,
            taps,
            conv_bias,
            bias_dt,
            log_rate,
        )
        if layer == 0:
            message = start_out(message)
        entry, gate = exchange_states(message, False, gate, complete_out if layer == 0 else None)
        (local,) = call(intra_kernel, [((rows, DI), F32)], [], place, act, step, cum, skip)
        mixed, gated_low = call(
            gate_kernel,
            [((rows, DI), F32), ((rows, DI), BF16)],
            [((rows, DI), F32)],
            place,
            entry,
            local,
            act,
            cum,
            gate,
            gain_gate,
        )
        own, rest = weights[2]
        first, second = split(gated_low)
        result = (hidden + dot(first, own[layer]) + dot(second, rest[layer])).astype(BF16)
        kept = (hidden, scale, normed_low, cd, edge, gate, pre, act, step, cum, entry, mixed, gated_low)
        return result, kept

    def columns_for(low, core, away):
        half = low.shape[1] // (2 * shards)
        return lax.dynamic_slice_in_dim(low, held_at(away, core) * half, half, 1)

    class Near:
        def __init__(self, product, low):
            self.product, self.low = product, low
            self.sent = [
                product(columns_for(low, 1 - section, away)).astype(BF16) for away in range(shards)
            ]

        def kept(self, away):
            part = self.product(columns_for(self.low, section, away))
            return part + turned(self.sent[away], "section", 1).astype(F32)

        def add_section(self):
            self.blocks = [self.kept(away).astype(BF16) for away in range(1, shards)]

        def send_shards(self):
            self.got = [turned(block, "wshard", away) for away, block in enumerate(self.blocks, 1)]

        def add_shards(self):
            total = self.kept(0)
            for block in self.got:
                total = total + block.astype(F32)
            return total.astype(BF16)

    def near_in(low, up):
        return Near(lambda columns: dot_tn(up, columns), low)

    def near_out(low, up):
        return Near(lambda columns: dot_tn(columns, up), low)

    lanes = D // (2 * shards)

    def lay_out(total):
        return jnp.concatenate(jnp.split(total, D // lanes, axis=1), axis=0)

    def layer_backward(layer, up_low, kept, beside, before=None, summing=None):
        gain_pre, taps, conv_bias, bias_dt, log_rate, skip, gain_gate = small_of(layer)
        hidden, scale, normed_low, cd, edge, gate, pre, act, step, cum, entry, mixed, gated_low = kept
        near = near_out(gated_low, up_low)
        own, rest = weights[2]
        grad_gated = jnp.concatenate([dot_nt(up_low, own[layer]), dot_nt(up_low, rest[layer])], axis=1)
        grad_gated, near.sent = together(grad_gated, near.sent)
        if before is not None:
            before.add_section()
            grad_gated, before.blocks = together(grad_gated, before.blocks)
        grad_mixed, grad_gate, grad_gain_gate, message = call(
            gate_back_kernel,
            [
                ((rows, DI), F32),
                ((rows, DI), BF16),
                ((1, DI), F32),
                ((N, MESSAGE), BF16),
            ],
            [((rows, DI), F32)],
            place,
            grad_gated,
            mixed,
            gate,
            gain_gate,
            cum,
            act,
        )
        near_gate = near_in(normed_low, grad_gate)
        near.add_section()
        grad_mixed, near_gate.sent, near.blocks = together(grad_mixed, near_gate.sent, near.blocks)
        near.send_shards()
        if before is not None:
            grad_mixed, near.got = together(grad_mixed, near.got)
            before.send_shards()
        grad_scaled, grad_bc, grad_cum = call(
            intra_back_kernel,
            [((rows, DI), F32), ((rows, 2 * N), F32), ((rows, H), F32)],
            [((rows, rows), F32), ((H, rows), F32)],
            place,
            act,
            step,
            cum,
            grad_mixed,
            entry,
        )
        held_back = () if summing is None else summing.moving
        leaving, (grad_scaled, held_back) = exchange_states(message, True, (grad_scaled, held_back))
        if summing is not None:
            summing.moving = held_back
            summing.scatter()
            grad_scaled, summing.split = together(grad_scaled, summing.split)
        near_gate.add_section()
        grad_scaled, near_gate.blocks, beside = together(grad_scaled, near_gate.blocks, beside)
        grad_cd, grad_tail, grad_edge, grad_taps, grad_conv_bias, grad_heads = call(
            finish_kernel,
            [
                ((rows, DCD), BF16),
                ((EDGE, DCONV), F32),
                ((EDGE, DCONV), F32),
                ((K, DCONV), F32),
                ((1, DCONV), F32),
                ((EDGE, H), F32),
            ],
            [((rows, DCONV), F32)],
            place,
            cd,
            edge,
            pre,
            act,
            step,
            cum,
            grad_mixed,
            grad_scaled,
            grad_bc,
            grad_cum,
            entry,
            leaving,
            taps,
            bias_dt,
            log_rate,
            skip,
        )
        edge_back = from_behind(grad_edge, -1)
        sum_out = lay_out(near.add_shards())
        if before is not None:
            sum_out = SeqSum(jnp.concatenate([sum_out, before.add_shards()], axis=0))
            summing.gather()
            edge_back, sum_out.sent, summing.copies = together(
                edge_back, sum_out.sent, summing.copies
            )
            sum_out.move()
        else:
            edge_back, sum_out = together(edge_back, sum_out)
        near_gate.send_shards()
        part_gate = near_gate.add_shards()
        edge_back, part_gate = together(edge_back, part_gate)
        grad_cd = lax.dynamic_update_slice(
            grad_cd, (grad_tail + edge_back).astype(BF16), (rows - EDGE, 0)
        )
        grad_normed = from_held(to_rows([(0, grad_cd), (1, grad_gate)], layer))
        grad_pulled = grad_normed * gain_pre
        cross = jnp.mean(grad_pulled * hidden, axis=-1, keepdims=True)
        grad_hidden = up_low.astype(F32) + scale * grad_pulled - scale**3 * cross * hidden
        grad_gain_pre = jnp.sum(grad_normed * hidden * scale, axis=0)
        small = (
            grad_gain_pre,
            grad_taps,
            grad_conv_bias,
            grad_heads[0],
            grad_heads[1],
            grad_heads[2],
            grad_gain_gate,
        )
        return grad_hidden, (sum_out, part_gate, grad_cd), small, beside

    middle, kept_first = layer_forward(0, source)
    ending, kept_second = layer_forward(1, middle)
    def placed(first, second):
        own = jnp.where(is_first, first, second)
        other = turned(jnp.where(is_first, second, first), "section", 1).astype(own.dtype)
        both = jnp.stack([jnp.where(is_first, own, other), jnp.where(is_first, other, own)])
        return both.reshape(1, batches, 1, rows, D)

    def placed_grads(first, second_low):
        own = jnp.where(is_first, first, second_low.astype(F32))
        sent = jnp.where(is_first, second_low, first.astype(BF16))
        other = turned(sent, "section", 1).astype(F32)
        both = jnp.stack([jnp.where(is_first, own, other), jnp.where(is_first, other, own)])
        return both.reshape(1, batches, 1, rows, D)

    grad_middle, (out_second, gate_second, grad_cd), small_second, acts = layer_backward(
        1, upstream, kept_second, placed(middle, ending)
    )
    grad_middle_low = grad_middle.astype(BF16)
    sums_second = jnp.concatenate([gate_second, out_second], axis=0)
    cd_second = near_in(kept_second[2], grad_cd)
    sums_second, grad_middle_low, cd_second.sent = together(
        sums_second, grad_middle_low, cd_second.sent
    )
    sums_second = SeqSum(sums_second).move()
    grad_source, (sums_out, gate_first, grad_cd), small_first, _ = layer_backward(
        0, grad_middle_low, kept_first, (), cd_second, sums_second
    )
    extra_rows = -(-sum(part.size for part in small_first) // (8 * 16 * lanes)) * 8 * 16

    def small_block(small):
        flat_grads = jnp.concatenate([part.reshape(-1) for part in small])
        flat_grads = jnp.pad(flat_grads, (0, extra_rows * lanes - flat_grads.size))
        return flat_grads.reshape(extra_rows, lanes)

    block_first, block_second = small_block(small_first), small_block(small_second)
    extra = jnp.where(is_first, block_first, block_second)
    extra_sent = jnp.where(is_first, block_second, block_first).astype(BF16)

    cd_first = near_in(kept_first[2], grad_cd)
    extra = extra + turned(extra_sent, "section", 1).astype(F32)
    sums_gate = SeqSum(gate_first).move()
    sums_out.scatter()
    cd_first.sent, sums_out.split = together(cd_first.sent, sums_out.split)
    sums_second.swap()
    cd_first.add_section()
    cd_first.blocks = [
        jnp.concatenate([block, extra.astype(BF16)], axis=0) for block in cd_first.blocks
    ]
    sums_second.own, cd_first.blocks = together(sums_second.own, cd_first.blocks)
    got_blocks = [turned(block, "wshard", away) for away, block in enumerate(cd_first.blocks, 1)]
    late = jnp.concatenate([cd_first.kept(0), extra], axis=0)
    late = (late + sum(block.astype(F32) for block in got_blocks)).astype(BF16)
    sums_gate.scatter()
    second = sums_second.whole()
    late, second, sums_gate.split = together(late, second, sums_gate.split)
    late = SeqSum(late).move()
    sums_out.gather()
    late.moving, sums_out.copies = together(late.moving, sums_out.copies)
    late.scatter()
    in_grad = placed_grads(grad_source, grad_middle_low)
    sums_out.swap()
    sums_out.own, late.split, in_grad = together(sums_out.own, late.split, in_grad)
    sums_gate.gather()
    late.gather()
    late.copies, sums_gate.copies = together(late.copies, sums_gate.copies)
    out_and_cd = sums_out.whole()
    sums_gate.swap()
    pick = section.astype(jnp.int32).reshape(1)

    def crossed(block, route):
        return [block, lax.ppermute(block, "section", route)]

    known = crossed(out_and_cd, [(0, 1), (1, 0)]) + crossed(second, [(0, 1)])
    (part_out,) = call(place_out_kernel, [((DI // shards, D), F32)], [], pick, *known)
    late.moving, part_out, known = together(late.moving, part_out, known)
    late.swap()
    gate_first, late_first = sums_gate.whole(), late.whole()
    (part_in,) = call(
        place_kernel,
        [((DI + DCD, 2 * lanes), F32)],
        [],
        pick,
        *crossed(gate_first, [(1, 0)]),
        *crossed(late_first, [(1, 0)]),
        *known,
    )
    mine = late_first[DCD:].astype(F32).reshape(-1)
    small_out, at = [], 0
    for part, shown in zip(small_first, small_parts):
        piece = mine[at : at + part.size].reshape(part.shape)
        at += part.size
        width = shown.shape[-1]
        piece = lax.dynamic_slice_in_dim(piece, shard * width, width, piece.ndim - 1)
        small_out.append(piece.reshape(shown.shape))
    return (
        acts,
        in_grad,
        small_out[0],
        jnp.swapaxes(part_in, 0, 1)[None],
        *small_out[1:],
        part_out[None],
    )


def solution(mesh):
    placed = (
        P(None, "wshard", "seq", None),
        P(None, "wshard", "seq", None),
        P(None, "wshard"),
        P("section", "wshard"),
        P("section", "wshard", None),
        P("section", None, "wshard"),
        P("section", "wshard"),
        P("section", "wshard"),
        P("section", "wshard"),
        P("section", "wshard"),
        P("section", "wshard"),
        P("section", "wshard", None),
    )
    return jax.shard_map(
        on_device,
        mesh=mesh,
        in_specs=placed,
        out_specs=(
            P("section", None, "wshard", "seq", None),
            P("section", None, "wshard", "seq", None),
            P("section", "wshard"),
            P("section", "wshard", None),
            P("section", None, "wshard"),
            P("section", "wshard"),
            P("section", "wshard"),
            P("section", "wshard"),
            P("section", "wshard"),
            P("section", "wshard"),
            P("section", "wshard", None),
        ),
        check_vma=False,
    )
```

```python
import jax
import jax.numpy as jnp
from jax import lax
from jax.experimental import pallas as pl
from jax.experimental.pallas import tpu as pltpu
from jax.sharding import PartitionSpec as P

D = 1024
DI = 2048
H = 32
HEAD = DI // H
N = 128
K = 4
DCONV = 2304
DCD = DCONV + H
PAIR = 2 * HEAD
WIDE = 512
BLOCK = 256
EDGE = 8
MESSAGE = DI + 128
EPSILON = 1e-05
LOG2E = 1.4426950408889634
FAR = -1e30
F32 = jnp.float32
BF16 = jnp.bfloat16
HIGH = lax.Precision.HIGHEST


def dot(a, b):
    return jnp.dot(a, b, preferred_element_type=F32)


def dot_nt(a, b):
    return lax.dot_general(a, b, (((1,), (1,)), ((), ())), preferred_element_type=F32)


def dot_tn(a, b):
    return lax.dot_general(a, b, (((0,), (0,)), ((), ())), preferred_element_type=F32)


def iota(shape, dim):
    return lax.broadcasted_iota(jnp.int32, shape, dim)


def ones_where(condition):
    return jnp.where(condition, 1.0, 0.0).astype(F32)


def two_parts(values):
    high = values.astype(BF16)
    return high, (values - high.astype(F32)).astype(BF16)


def spread(values, start, width):
    pick = ones_where((start + iota((H, width), 1)) // HEAD == iota((H, width), 0)).astype(BF16)
    high, low = two_parts(values)
    return dot(high, pick) + dot(low, pick)


def head_sums(values, start):
    width = values.shape[1]
    pick = ones_where((start + iota((width, H), 0)) // HEAD == iota((width, H), 1)).astype(BF16)
    high, low = two_parts(values)
    return dot(high, pick) + dot(low, pick)


def sigmoid(values):
    return 0.5 * jnp.tanh(0.5 * values) + 0.5


def rows_of_one(row):
    return jnp.broadcast_to(row, (EDGE, row.shape[1]))


def segments(place, rows):
    offset, bound = place[0], place[1]
    position = offset + iota((rows, 1), 0)
    segment = ones_where(position >= bound)
    before = jnp.where(offset - 1 >= bound, 1.0, 0.0).astype(F32)
    last = jnp.where(offset + rows - 1 >= bound, 1.0, 0.0).astype(F32)
    return position, segment, before, last


def tap_masks(place, position):
    bound = place[1]
    return [
        ones_where((position - back >= bound) == (position >= bound)) if back else None
        for back in range(K)
    ]


def decay_lanes(through):
    high, low = two_parts(jnp.broadcast_to(through, (N, H)))
    first = ones_where(iota((H, 128), 0) == iota((H, 128), 1)).astype(BF16)
    second = ones_where(iota((H, 128), 0) + H == iota((H, 128), 1)).astype(BF16)
    return dot(high, first) + dot(low, second)


def states_kernel(place, cd, edge, conv_w, conv_b, dt_bias, a_log, pre, act, step, cum, message):
    rows = cd.shape[0]
    position, segment, before, last = segments(place, rows)
    masks = tap_masks(place, position)
    step_now = jax.nn.softplus(cd[:, DCONV:] + dt_bias[...])
    log_decay = -step_now * jnp.exp(a_log[...])
    lower = ones_where(iota((rows, rows), 0) >= iota((rows, rows), 1))
    summed = jnp.dot(lower, log_decay, precision=HIGH, preferred_element_type=F32)
    step[...] = step_now
    cum[...] = summed
    total = summed[rows - 1 :, :]
    weight = step_now * jnp.where(segment == last, jnp.exp(total - summed), 0.0)
    for start in range(0, DCONV, BLOCK):
        here = slice(start, start + BLOCK)
        values = cd[:, here]
        extended = jnp.concatenate([edge[:, here], values], axis=0)
        conv = conv_b[:, here] + conv_w[K - 1 : K, here] * values
        for back in range(1, K):
            moved = pltpu.roll(extended, back, 0)[EDGE:]
            conv = conv + conv_w[K - 1 - back : K - back, here] * moved * masks[back]
        pre[:, here] = conv
        act[:, here] = conv * sigmoid(conv)
    in_high, in_low = two_parts(jnp.transpose(act[:, DI : DI + N]))
    for start in range(0, DI, WIDE):
        here = slice(start, start + WIDE)
        high, low = two_parts(act[:, here] * spread(weight, start, WIDE))
        message[:, here] = dot(in_high, high) + dot(in_high, low) + dot(in_low, high)
    through = jnp.exp(total) * jnp.where(before == last, 1.0, 0.0)
    message[:, DI:] = decay_lanes(through).astype(message.dtype)


def carry_kernel(reverse, gathered, out, *scratch):
    count, rows = gathered.shape[0], gathered.shape[1]
    pick = ones_where(iota((2 * H, DI), 1) // HEAD == iota((2 * H, DI), 0) % H).astype(BF16)
    state = jnp.zeros((rows, DI), F32)
    for source in range(count - 1, -1, -1) if reverse else range(count):
        out[source] = state.astype(out.dtype)
        part = gathered[source]
        through = dot(part[:, DI : DI + 2 * H].astype(BF16), pick)
        state = through * state + part[:, :DI].astype(F32)


def intra_kernel(place, act, step, cum, skip, local):
    rows = act.shape[0]
    position, segment, _, _ = segments(place, rows)
    scores = lax.dot_general(
        act[:, DI + N :],
        act[:, DI : DI + N],
        (((1,), (1,)), ((), ())),
        precision=HIGH,
        preferred_element_type=F32,
    )
    across = place[0] + iota((1, rows), 1)
    same = segment == ones_where(across >= place[1])
    bias = jnp.where((position >= across) & same, 0.0, FAR)
    level = cum[...] * LOG2E
    level_t = jnp.transpose(level)
    steps = step[...]
    skips = rows_of_one(skip[...])
    half = rows // 2
    left = iota((rows, PAIR), 1) < HEAD
    for pair in range(H // 2):
        start = pair * PAIR
        here = slice(start, start + PAIR)
        values = act[:, here]
        high, low = two_parts(values * spread(steps, start, PAIR))
        scaled = jnp.concatenate([high, low], axis=1)
        outs = []
        for head in (2 * pair, 2 * pair + 1):
            parts = []
            for top, until in ((0, half), (half, rows)):
                here_rows = slice(top, top + half)
                decay = jnp.exp2(
                    level[here_rows, head : head + 1]
                    - level_t[head : head + 1, :until]
                    + bias[here_rows, :until]
                )
                first, second = two_parts(decay * scores[here_rows, :until])
                both = dot(first, scaled[:until])
                parts.append(both[:, :PAIR] + both[:, PAIR:] + dot(second, high[:until]))
            outs.append(jnp.concatenate(parts, axis=0))
        local[:, here] = jnp.where(left, outs[0], outs[1]) + spread(skips, start, PAIR)[:1] * values


def gate_kernel(place, entry, local, act, cum, gate, gain, mixed, gated, kept):
    rows = act.shape[0]
    _, segment, before, _ = segments(place, rows)
    enter = jnp.exp(cum[...]) * ones_where(segment == before)
    out_high, out_low = two_parts(act[:, DI + N :])
    square = jnp.zeros((rows, 1), F32)
    for start in range(0, DI, WIDE):
        here = slice(start, start + WIDE)
        high, low = two_parts(entry[:, here])
        entered = dot(out_high, high) + dot(out_low, high) + dot(out_high, low)
        y = local[:, here] + entered * spread(enter, start, WIDE)
        mixed[:, here] = y
        raw = gate[:, here]
        u = y * raw * sigmoid(raw)
        kept[:, here] = u
        square = square + jnp.sum(u * u, axis=1, keepdims=True)
    scale = lax.rsqrt(square / DI + EPSILON)
    count = place.shape[0] - 2
    width = DI // count
    for group in range(count):
        here = slice(group * width, (group + 1) * width)
        there = pl.ds(pl.multiple_of(place[2 + group], 128), width)
        gated[:, there] = (kept[:, here] * scale * gain[:, here]).astype(BF16)


def gate_back_kernel(
    place, grad_gated, mixed, gate, gain, cum, act, grad_mixed, grad_gate, grad_gain, message, kept
):
    rows = act.shape[0]
    _, segment, before, last = segments(place, rows)
    summed = cum[...]
    enter = jnp.exp(summed) * ones_where(segment == before)
    out_t = jnp.transpose(act[:, DI + N :]).astype(BF16)
    square = jnp.zeros((rows, 1), F32)
    cross = jnp.zeros((rows, 1), F32)
    count = place.shape[0] - 2
    width = DI // count
    for group in range(count):
        here = slice(group * width, (group + 1) * width)
        there = pl.ds(pl.multiple_of(place[2 + group], 128), width)
        raw = gate[:, here]
        u = mixed[:, here] * raw * sigmoid(raw)
        kept[:, here] = u
        square = square + jnp.sum(u * u, axis=1, keepdims=True)
        cross = cross + jnp.sum(grad_gated[:, there] * gain[:, here] * u, axis=1, keepdims=True)
    scale = lax.rsqrt(square / DI + EPSILON)
    pulled = scale * scale * scale * cross / DI
    for group in range(count):
        start = group * width
        here = slice(start, start + width)
        there = pl.ds(pl.multiple_of(place[2 + group], 128), width)
        raw = gate[:, here]
        u = kept[:, here]
        up = grad_gated[:, there]
        grad_gain[:, here] = jnp.sum(up * u * scale, axis=0, keepdims=True)
        grad_u = scale * up * gain[:, here] - pulled * u
        curve = sigmoid(raw)
        grad_y = grad_u * raw * curve
        grad_gate[:, here] = (
            grad_u * mixed[:, here] * curve * (1.0 + raw * (1.0 - curve))
        ).astype(BF16)
        grad_mixed[:, here] = grad_y
        pull = (grad_y * spread(enter, start, width)).astype(BF16)
        message[:, here] = dot(out_t, pull).astype(BF16)
    through = jnp.exp(summed[rows - 1 :, :]) * jnp.where(before == last, 1.0, 0.0)
    message[:, DI:] = decay_lanes(through).astype(message.dtype)


def intra_back_kernel(
    place, act, step, cum, grad_mixed, entry, grad_scaled, grad_bc, grad_cum, grad_scores, across_sum
):
    rows = act.shape[0]
    position, segment, before, _ = segments(place, rows)
    in_b = act[:, DI : DI + N].astype(BF16)
    out_c = act[:, DI + N :].astype(BF16)
    scores = dot_nt(in_b, out_c)
    across = place[0] + iota((1, rows), 1)
    same = segment == ones_where(across >= place[1])
    bias = jnp.where((across >= position) & same, 0.0, FAR)
    summed = cum[...]
    level = summed * LOG2E
    level_t = jnp.transpose(level)
    steps = step[...]
    left = iota((rows, PAIR), 1) < HEAD
    lane = iota((rows, H), 1)
    half = rows // 2
    grad_scores[...] = jnp.zeros((rows, rows), F32)
    down_sum = jnp.zeros((rows, H), F32)
    for pair in range(H // 2):
        start = pair * PAIR
        here = slice(start, start + PAIR)
        scaled = act[:, here] * spread(steps, start, PAIR)
        up = grad_mixed[:, here].astype(BF16)
        outs = []
        for head in (2 * pair, 2 * pair + 1):
            mine = left if head % 2 == 0 else jnp.logical_not(left)
            own = jnp.where(mine, scaled, 0.0).astype(BF16)
            parts, sums = [], []
            for top in (0, half):
                here_rows = slice(top, top + half)
                grad_weight = dot_nt(own[here_rows], up[top:])
                decay = jnp.exp2(
                    level_t[head : head + 1, top:]
                    - level[here_rows, head : head + 1]
                    + bias[here_rows, top:]
                )
                weight = decay * scores[here_rows, top:]
                grad_scores[here_rows, top:] += decay * grad_weight
                flow = weight * grad_weight
                if top == 0:
                    across_sum[head : head + 1, :] = jnp.sum(flow, axis=0, keepdims=True)
                else:
                    across_sum[head : head + 1, top:] += jnp.sum(flow, axis=0, keepdims=True)
                sums.append(jnp.sum(flow, axis=1, keepdims=True))
                parts.append(dot(weight.astype(BF16), up[top:]))
            down_sum = down_sum + jnp.where(lane == head, jnp.concatenate(sums, axis=0), 0.0)
            outs.append(jnp.concatenate(parts, axis=0))
        grad_scaled[:, here] = jnp.where(left, outs[0], outs[1])
    enter = jnp.exp(summed) * ones_where(segment == before)
    grad_out = jnp.zeros((rows, N), F32)
    grad_enter = jnp.zeros((rows, H), F32)
    for start in range(0, DI, WIDE):
        here = slice(start, start + WIDE)
        entered = entry[:, here].astype(BF16)
        pull = grad_mixed[:, here] * spread(enter, start, WIDE)
        grad_out = grad_out + dot_nt(pull.astype(BF16), entered)
        grad_enter = grad_enter + head_sums(pull * dot(out_c, entered), start)
    low = grad_scores[...].astype(BF16)
    grad_bc[:, :N] = dot(low, out_c)
    grad_bc[:, N:] = grad_out + dot(jnp.transpose(grad_scores[...]).astype(BF16), in_b)
    grad_cum[...] = jnp.transpose(across_sum[...]) - down_sum + grad_enter


def finish_kernel(
    place,
    cd,
    edge,
    pre,
    act,
    step,
    cum,
    grad_mixed,
    grad_scaled,
    grad_bc,
    grad_cum,
    entry,
    leaving,
    conv_w,
    dt_bias,
    a_log,
    skip,
    grad_cd,
    grad_tail,
    grad_edge,
    grad_conv_w,
    grad_conv_b,
    grad_heads,
    grad_pre,
):
    rows = cd.shape[0]
    position, segment, before, last = segments(place, rows)
    masks = tap_masks(place, position)
    summed = cum[...]
    total = summed[rows - 1 :, :]
    to_end = jnp.where(segment == last, jnp.exp(total - summed), 0.0)
    steps = step[...]
    skips = rows_of_one(skip[...])
    in_b = act[:, DI : DI + N].astype(BF16)

    def silu_slope(values):
        curve = sigmoid(values)
        return curve * (1.0 + values * (1.0 - curve))

    grad_end = jnp.zeros((rows, H), F32)
    grad_step = jnp.zeros((rows, H), F32)
    grad_in = grad_bc[:, :N]
    grad_through = jnp.zeros((EDGE, H), F32)
    grad_skip = jnp.zeros((EDGE, H), F32)
    for start in range(0, DI, WIDE):
        here = slice(start, start + WIDE)
        values = act[:, here]
        up = grad_mixed[:, here]
        left = leaving[:, here]
        step_wide = spread(steps, start, WIDE)
        end_wide = spread(to_end, start, WIDE)
        pulled = dot(in_b, left) * end_wide
        scaled = values * step_wide
        grad_now = grad_scaled[:, here] + pulled
        grad_end = grad_end + head_sums(scaled * pulled, start)
        grad_step = grad_step + head_sums(grad_now * values, start)
        grad_in = grad_in + dot_nt((end_wide * scaled).astype(BF16), left)
        states = jnp.sum(entry[:, here].astype(F32) * left.astype(F32), axis=0, keepdims=True)
        grad_through = grad_through + head_sums(rows_of_one(states), start)
        skipped = jnp.sum(up * values, axis=0, keepdims=True)
        grad_skip = grad_skip + head_sums(rows_of_one(skipped), start)
        grad_x = grad_now * step_wide + spread(skips, start, WIDE)[:1] * up
        grad_pre[:, here] = grad_x * silu_slope(pre[:, here])
    grad_pre[:, DI : DI + N] = grad_in * silu_slope(pre[:, DI : DI + N])
    grad_pre[:, DI + N :] = grad_bc[:, N:] * silu_slope(pre[:, DI + N :])
    through = jnp.exp(total) * jnp.where(before == last, 1.0, 0.0)
    at_last = jnp.sum(grad_end, axis=0, keepdims=True) + through * grad_through[:1]
    upper = ones_where(iota((rows, rows), 1) >= iota((rows, rows), 0))
    grad_log = at_last + jnp.dot(
        upper, grad_cum[...] - grad_end, precision=HIGH, preferred_element_type=F32
    )
    rate = jnp.exp(a_log[...])
    grad_step = grad_step - rate * grad_log
    grad_raw = grad_step * sigmoid(cd[:, DCONV:] + dt_bias[...])
    grad_cd[:, DCONV:] = grad_raw.astype(BF16)
    grad_heads[0:1, :] = jnp.sum(grad_raw, axis=0, keepdims=True)
    grad_heads[1:2, :] = jnp.sum(grad_log * -steps * rate, axis=0, keepdims=True)
    grad_heads[2:3, :] = grad_skip[:1]
    grad_heads[3:, :] = jnp.zeros((EDGE - 3, H), F32)
    nothing = jnp.zeros((EDGE, BLOCK), F32)
    for start in range(0, DCONV, BLOCK):
        here = slice(start, start + BLOCK)
        values = cd[:, here]
        extended = jnp.concatenate([edge[:, here], values], axis=0)
        up = grad_pre[:, here]
        grad_conv_b[:, here] = jnp.sum(up, axis=0, keepdims=True)
        grad_conv_w[K - 1 : K, here] = jnp.sum(up * values, axis=0, keepdims=True)
        spilled = nothing
        grad_in_now = conv_w[K - 1 : K, here] * up
        for back in range(1, K):
            moved = pltpu.roll(extended, back, 0)[EDGE:]
            masked = up * masks[back]
            grad_conv_w[K - 1 - back : K - back, here] = jnp.sum(
                masked * moved, axis=0, keepdims=True
            )
            framed = jnp.concatenate([nothing, masked, nothing], axis=0)
            returned = pltpu.roll(framed, rows + 2 * EDGE - back, 0)
            tap = conv_w[K - 1 - back : K - back, here]
            spilled = spilled + tap * returned[:EDGE]
            grad_in_now = grad_in_now + tap * returned[EDGE : EDGE + rows]
        grad_edge[:, here] = spilled
        grad_tail[:, here] = grad_in_now[rows - EDGE :]
        grad_cd[:, here] = grad_in_now.astype(BF16)


def place_kernel(
    pick, gate, gate_other, late, late_other, out_and_cd, out_and_cd_other, second, second_other, out
):
    rows, lanes = gate.shape
    rest = out.shape[0] - rows

    @pl.when(pick[0] == 0)
    def _():
        out[:rows, :lanes] = gate[...].astype(F32)
        out[:rows, lanes:] = gate_other[...].astype(F32)
        out[rows:, :lanes] = late[:rest, :].astype(F32)
        out[rows:, lanes:] = late_other[:rest, :].astype(F32)

    @pl.when(pick[0] != 0)
    def _():
        out[:rows, :lanes] = second_other[:rows, :].astype(F32)
        out[:rows, lanes:] = second[:rows, :].astype(F32)
        out[rows:, :lanes] = out_and_cd_other[DI:, :].astype(F32)
        out[rows:, lanes:] = out_and_cd[DI:, :].astype(F32)


def place_out_kernel(pick, first, first_other, second, second_other, out):
    lanes = first.shape[1]
    half = out.shape[0] // 2

    def write(at, block, start):
        for column in range(out.shape[1] // lanes):
            out[at : at + half, column * lanes : (column + 1) * lanes] = block[
                start + column * half : start + (column + 1) * half, :
            ].astype(F32)

    @pl.when(pick[0] == 0)
    def _():
        write(0, first, 0)
        write(half, first_other, 0)

    @pl.when(pick[0] != 0)
    def _():
        write(0, second_other, DI)
        write(half, second, DI)


def call(body, outs, scratch, *operands):
    whole = pl.BlockSpec(memory_space=pltpu.VMEM)
    scalars = [pl.BlockSpec(memory_space=pltpu.SMEM)] if operands[0].dtype == jnp.int32 else []
    return pl.pallas_call(
        body,
        out_shape=[jax.ShapeDtypeStruct(shape, kind) for shape, kind in outs],
        in_specs=scalars + [whole] * (len(operands) - len(scalars)),
        out_specs=[whole] * len(outs),
        scratch_shapes=[pltpu.VMEM(shape, kind) for shape, kind in scratch],
        compiler_params=pltpu.CompilerParams(vmem_limit_bytes=56 * 1024 * 1024),
    )(*operands)


def turned(block, axis, distance):
    count = lax.axis_size(axis)
    return lax.ppermute(block, axis, [(i, (i + distance) % count) for i in range(count)])


def from_behind(block, distance):
    count = lax.axis_size("seq")
    route = [(i - distance, i) for i in range(count) if 0 <= i - distance < count]
    return lax.ppermute(block, "seq", route)


def together(*values):
    return lax.optimization_barrier(values)


def neighbours():
    return [(i, i ^ 1) for i in range(lax.axis_size("seq"))]


def exchange_states(message, reverse, beside, then=None):
    count = lax.axis_size("seq")
    rows = N // count
    sent = message.reshape(count, rows, MESSAGE)
    gathered = lax.all_to_all(sent, "seq", 0, 0)
    gathered, beside = together(gathered, beside)

    def body(gathered_ref, out_ref):
        carry_kernel(reverse, gathered_ref, out_ref)

    (states,) = call(body, [((count, rows, DI), message.dtype)], [], gathered)
    if then is not None:
        states = then(states)
    return lax.all_to_all(states, "seq", 0, 0).reshape(N, DI), beside


class SeqSum:
    def __init__(self, part):
        count = lax.axis_size("seq")
        self.parity = lax.axis_index("seq") % 2
        self.others = count // 2
        self.groups = [[2 * i + p for i in range(self.others)] for p in range(2)]
        self.half, self.lanes = part.shape[0] // 2, part.shape[1]
        self.keep = lax.dynamic_slice_in_dim(part, self.parity * self.half, self.half, 0)
        self.sent = lax.dynamic_slice_in_dim(part, (1 - self.parity) * self.half, self.half, 0)

    def move(self):
        self.moving = lax.ppermute(self.sent, "seq", neighbours())
        return self

    def over_others(self, split):
        return lax.all_to_all(split, "seq", 0, 0, axis_index_groups=self.groups)

    def scatter(self):
        both = (self.keep.astype(F32) + self.moving.astype(F32)).astype(BF16)
        self.split = both.reshape(self.others, self.half // self.others, self.lanes)
        self.moving = self.over_others(self.split)

    def gather(self):
        total = jnp.sum(self.moving.astype(F32), axis=0).astype(BF16)
        self.copies = jnp.broadcast_to(total, (self.others,) + total.shape)
        self.moving = self.over_others(self.copies)

    def swap(self):
        self.own = self.moving.reshape(self.half, self.lanes)
        self.moving = lax.ppermute(self.own, "seq", neighbours())

    def whole(self):
        return jnp.where(
            self.parity == 0,
            jnp.concatenate([self.own, self.moving], axis=0),
            jnp.concatenate([self.moving, self.own], axis=0),
        )


def on_device(
    inputs,
    cotangent,
    boundary,
    norm_gain,
    w_in,
    conv_w,
    conv_b,
    dt_bias,
    a_log,
    skip_gain,
    gate_norm,
    w_out,
):
    section = lax.axis_index("section")
    sections = lax.axis_size("section")
    shard = lax.axis_index("wshard")
    shards = lax.axis_size("wshard")
    parity = lax.axis_index("seq") % 2
    batches, _, rows, _ = inputs.shape
    is_first = section == 0

    offset = lax.axis_index("seq") * rows
    source = lax.dynamic_index_in_dim(inputs[:, 0], section, keepdims=False)
    upstream = lax.dynamic_index_in_dim(cotangent[:, 0], section, keepdims=False)
    bound = lax.dynamic_index_in_dim(boundary[:, 0], section, keepdims=False)

    def held_at(away, which):
        return 2 * away + (which + (parity if away else 0)) % 2

    def held_halves():
        out = []
        for away in range(shards):
            for half in range(2):
                which = (half + (parity if away else 0)) % 2
                out.append(2 * ((shard + away) % shards) + which)
        return out

    held = held_halves()

    def to_held(values):
        half = values.shape[1] // (2 * shards)
        own = lax.dynamic_slice_in_dim(values, held[0] * half, 2 * half, 1)
        rest = [lax.dynamic_slice_in_dim(values, at * half, half, 1) for at in held[2:]]
        return jnp.concatenate([own] + rest, axis=1)

    def from_held(values):
        half = values.shape[1] // (2 * shards)
        out = jnp.zeros(values.shape, values.dtype)
        out = lax.dynamic_update_slice_in_dim(out, values[:, : 2 * half], held[0] * half, 1)
        for place_held, at in enumerate(held[2:], 2):
            piece = values[:, place_held * half : (place_held + 1) * half]
            out = lax.dynamic_update_slice_in_dim(out, piece, at * half, 1)
        return out

    half_out = DI // (2 * shards)
    held_starts = []
    for block in range(shards):
        away = (block - shard) % shards
        for which in range(2):
            turn = jnp.where(away == 0, 0, parity)
            held_starts.append((2 * away + (which + turn) % 2) * half_out)
    place = jnp.stack([offset, bound] + held_starts).astype(jnp.int32)

    small_parts = (norm_gain, conv_w, conv_b, dt_bias, a_log, skip_gain, gate_norm)
    flat = jnp.concatenate([part.reshape(-1) for part in small_parts])
    flats = jnp.stack([flat] + [turned(flat, "wshard", -away) for away in range(1, shards)])
    flats = jnp.concatenate([flats, flats], axis=0)
    flats = lax.dynamic_slice_in_dim(flats, (shards - shard) % shards, shards, 0)
    flats_other = turned(flats, "section", 1)

    turned_in = jnp.swapaxes(w_in[0], 0, 1)
    own_pieces = [(turned_in[DI:], 1), (turned_in[:DI], 1), (w_out[0], 0)]
    halves = [
        lax.dynamic_slice_in_dim(own, parity * own.shape[dim] // 2, own.shape[dim] // 2, dim)
        for own, dim in own_pieces
    ]

    def fetch(sent):
        return [turned(sent, "wshard", -away) for away in range(1, shards)]

    def beside(got):
        return [lax.ppermute(block, "seq", neighbours()) for block in got]

    def joined(which, got, other):
        pairs = [block for pair in zip(got, other) for block in pair]
        return lax.all_gather(jnp.concatenate(pairs, axis=own_pieces[which][1]), "section")

    weights = [[lax.all_gather(own, "section"), None] for own, _ in own_pieces]
    cut = DCD // 2
    got_cd = fetch(halves[0][:cut])
    sent_cd, got_cd = together(halves[0][cut:], got_cd)
    got_cd_rest = fetch(sent_cd)
    other_cd = beside(got_cd)
    sent_gate, got_cd_rest, other_cd, flats, flats_other = together(
        halves[1], got_cd_rest, other_cd, flats, flats_other
    )
    got_gate = fetch(sent_gate)
    other_cd_rest = beside(got_cd_rest)
    other_cd, other_cd_rest = together(other_cd, other_cd_rest)

    def stacked(first, second):
        return [jnp.concatenate([a, b], axis=0) for a, b in zip(first, second)]

    got_cd, other_cd = stacked(got_cd, got_cd_rest), stacked(other_cd, other_cd_rest)
    got_gate, other_cd = lax.optimization_barrier((got_gate, other_cd))
    weights[0][1] = joined(0, got_cd, other_cd)
    other_gate = beside(got_gate)
    sent_out, got_gate = together(halves[2], got_gate)
    got_out = fetch(sent_out)

    def complete_gate(cd):
        cd, got, other = together(cd, got_gate, other_gate)
        weights[1][1] = joined(1, got, other)
        return cd

    def start_out(event):
        got, event = together(got_out, event)
        weights[2][1] = (got, beside(got))
        return event

    def complete_out(event):
        got, other = weights[2][1]
        got, other, event = together(got, other, event)
        weights[2][1] = joined(2, got, other)
        return event

    def split(values):
        cut = values.shape[1] // shards
        return values[:, :cut], values[:, cut:]

    def from_rows(which, layer, values):
        own, rest = weights[which]
        first, second = split(values)
        return dot_nt(first, own[layer]) + dot_nt(second, rest[layer])

    def to_rows(terms, layer):
        own = sum(dot(values, weights[which][0][layer]) for which, values in terms)
        rest = sum(dot(values, weights[which][1][layer]) for which, values in terms)
        return jnp.concatenate([own, rest], axis=1)

    def small_of(layer):
        every = jnp.where(section == layer, flats, flats_other)
        out, at = [], 0
        for part in small_parts:
            size = part.size
            piece = every[:, at : at + size].reshape((shards,) + part.shape[1:])
            at += size
            if part.ndim == 3:
                out.append(jnp.moveaxis(piece, 0, 1).reshape(part.shape[1], -1))
            else:
                out.append(piece.reshape(1, -1))
        return out

    def layer_forward(layer, hidden_low):
        gain_pre, taps, conv_bias, bias_dt, log_rate, skip, gain_gate = small_of(layer)
        hidden = hidden_low.astype(F32)
        scale = lax.rsqrt(jnp.mean(hidden * hidden, axis=-1, keepdims=True) + EPSILON)
        normed_low = to_held((hidden * scale * gain_pre).astype(BF16))
        cd = from_rows(0, layer, normed_low)
        if layer == 0:
            cd = complete_gate(cd)
        edge = from_behind(cd[rows - EDGE :, :DCONV], 1)
        gate = from_rows(1, layer, normed_low)
        pre, act, step, cum, message = call(
            states_kernel,
            [
                ((rows, DCONV), F32),
                ((rows, DCONV), F32),
                ((rows, H), F32),
                ((rows, H), F32),
                ((N, MESSAGE), F32),
            ],
            [],
            place,
            cd,
            edge,
            taps,
            conv_bias,
            bias_dt,
            log_rate,
        )
        if layer == 0:
            message = start_out(message)
        entry, gate = exchange_states(message, False, gate, complete_out if layer == 0 else None)
        (local,) = call(intra_kernel, [((rows, DI), F32)], [], place, act, step, cum, skip)
        mixed, gated_low = call(
            gate_kernel,
            [((rows, DI), F32), ((rows, DI), BF16)],
            [((rows, DI), F32)],
            place,
            entry,
            local,
            act,
            cum,
            gate,
            gain_gate,
        )
        own, rest = weights[2]
        first, second = split(gated_low)
        result = (hidden + dot(first, own[layer]) + dot(second, rest[layer])).astype(BF16)
        kept = (hidden, scale, normed_low, cd, edge, gate, pre, act, step, cum, entry, mixed, gated_low)
        return result, kept

    def columns_for(low, core, away):
        half = low.shape[1] // (2 * shards)
        return lax.dynamic_slice_in_dim(low, held_at(away, core) * half, half, 1)

    class Near:
        def __init__(self, product, low):
            self.product, self.low = product, low
            self.sent = [
                product(columns_for(low, 1 - section, away)).astype(BF16) for away in range(shards)
            ]

        def kept(self, away):
            part = self.product(columns_for(self.low, section, away))
            return part + turned(self.sent[away], "section", 1).astype(F32)

        def add_section(self):
            self.blocks = [self.kept(away).astype(BF16) for away in range(1, shards)]

        def send_shards(self):
            self.got = [turned(block, "wshard", away) for away, block in enumerate(self.blocks, 1)]

        def add_shards(self):
            total = self.kept(0)
            for block in self.got:
                total = total + block.astype(F32)
            return total.astype(BF16)

    def near_in(low, up):
        return Near(lambda columns: dot_tn(up, columns), low)

    def near_out(low, up):
        return Near(lambda columns: dot_tn(columns, up), low)

    lanes = D // (2 * shards)

    def lay_out(total):
        return jnp.concatenate(jnp.split(total, D // lanes, axis=1), axis=0)

    def layer_backward(layer, up_low, kept, beside, before=None, summing=None):
        gain_pre, taps, conv_bias, bias_dt, log_rate, skip, gain_gate = small_of(layer)
        hidden, scale, normed_low, cd, edge, gate, pre, act, step, cum, entry, mixed, gated_low = kept
        near = near_out(gated_low, up_low)
        own, rest = weights[2]
        grad_gated = jnp.concatenate([dot_nt(up_low, own[layer]), dot_nt(up_low, rest[layer])], axis=1)
        grad_gated, near.sent = together(grad_gated, near.sent)
        if before is not None:
            before.add_section()
            grad_gated, before.blocks = together(grad_gated, before.blocks)
        grad_mixed, grad_gate, grad_gain_gate, message = call(
            gate_back_kernel,
            [
                ((rows, DI), F32),
                ((rows, DI), BF16),
                ((1, DI), F32),
                ((N, MESSAGE), BF16),
            ],
            [((rows, DI), F32)],
            place,
            grad_gated,
            mixed,
            gate,
            gain_gate,
            cum,
            act,
        )
        near_gate = near_in(normed_low, grad_gate)
        near.add_section()
        grad_mixed, near_gate.sent, near.blocks = together(grad_mixed, near_gate.sent, near.blocks)
        near.send_shards()
        if before is not None:
            grad_mixed, near.got = together(grad_mixed, near.got)
            before.send_shards()
        grad_scaled, grad_bc, grad_cum = call(
            intra_back_kernel,
            [((rows, DI), F32), ((rows, 2 * N), F32), ((rows, H), F32)],
            [((rows, rows), F32), ((H, rows), F32)],
            place,
            act,
            step,
            cum,
            grad_mixed,
            entry,
        )
        held_back = () if summing is None else summing.moving
        leaving, (grad_scaled, held_back) = exchange_states(message, True, (grad_scaled, held_back))
        if summing is not None:
            summing.moving = held_back
            summing.scatter()
            grad_scaled, summing.split = together(grad_scaled, summing.split)
        near_gate.add_section()
        grad_scaled, near_gate.blocks, beside = together(grad_scaled, near_gate.blocks, beside)
        grad_cd, grad_tail, grad_edge, grad_taps, grad_conv_bias, grad_heads = call(
            finish_kernel,
            [
                ((rows, DCD), BF16),
                ((EDGE, DCONV), F32),
                ((EDGE, DCONV), F32),
                ((K, DCONV), F32),
                ((1, DCONV), F32),
                ((EDGE, H), F32),
            ],
            [((rows, DCONV), F32)],
            place,
            cd,
            edge,
            pre,
            act,
            step,
            cum,
            grad_mixed,
            grad_scaled,
            grad_bc,
            grad_cum,
            entry,
            leaving,
            taps,
            bias_dt,
            log_rate,
            skip,
        )
        edge_back = from_behind(grad_edge, -1)
        sum_out = lay_out(near.add_shards())
        if before is not None:
            sum_out = SeqSum(jnp.concatenate([sum_out, before.add_shards()], axis=0))
            summing.gather()
            edge_back, sum_out.sent, summing.copies = together(
                edge_back, sum_out.sent, summing.copies
            )
            sum_out.move()
        else:
            edge_back, sum_out = together(edge_back, sum_out)
        near_gate.send_shards()
        part_gate = near_gate.add_shards()
        edge_back, part_gate = together(edge_back, part_gate)
        grad_cd = lax.dynamic_update_slice(
            grad_cd, (grad_tail + edge_back).astype(BF16), (rows - EDGE, 0)
        )
        grad_normed = from_held(to_rows([(0, grad_cd), (1, grad_gate)], layer))
        grad_pulled = grad_normed * gain_pre
        cross = jnp.mean(grad_pulled * hidden, axis=-1, keepdims=True)
        grad_hidden = up_low.astype(F32) + scale * grad_pulled - scale**3 * cross * hidden
        grad_gain_pre = jnp.sum(grad_normed * hidden * scale, axis=0)
        small = (
            grad_gain_pre,
            grad_taps,
            grad_conv_bias,
            grad_heads[0],
            grad_heads[1],
            grad_heads[2],
            grad_gain_gate,
        )
        return grad_hidden, (sum_out, part_gate, grad_cd), small, beside

    middle, kept_first = layer_forward(0, source)
    ending, kept_second = layer_forward(1, middle)
    def placed(first, second):
        own = jnp.where(is_first, first, second)
        other = turned(jnp.where(is_first, second, first), "section", 1).astype(own.dtype)
        both = jnp.stack([jnp.where(is_first, own, other), jnp.where(is_first, other, own)])
        return both.reshape(1, batches, 1, rows, D)

    def placed_grads(first, second_low):
        own = jnp.where(is_first, first, second_low.astype(F32))
        sent = jnp.where(is_first, second_low, first.astype(BF16))
        other = turned(sent, "section", 1).astype(F32)
        both = jnp.stack([jnp.where(is_first, own, other), jnp.where(is_first, other, own)])
        return both.reshape(1, batches, 1, rows, D)

    grad_middle, (out_second, gate_second, grad_cd), small_second, acts = layer_backward(
        1, upstream, kept_second, placed(middle, ending)
    )
    grad_middle_low = grad_middle.astype(BF16)
    sums_second = jnp.concatenate([gate_second, out_second], axis=0)
    cd_second = near_in(kept_second[2], grad_cd)
    sums_second, grad_middle_low, cd_second.sent = together(
        sums_second, grad_middle_low, cd_second.sent
    )
    sums_second = SeqSum(sums_second).move()
    grad_source, (sums_out, gate_first, grad_cd), small_first, _ = layer_backward(
        0, grad_middle_low, kept_first, (), cd_second, sums_second
    )
    extra_rows = -(-sum(part.size for part in small_first) // (8 * 16 * lanes)) * 8 * 16

    def small_block(small):
        flat_grads = jnp.concatenate([part.reshape(-1) for part in small])
        flat_grads = jnp.pad(flat_grads, (0, extra_rows * lanes - flat_grads.size))
        return flat_grads.reshape(extra_rows, lanes)

    block_first, block_second = small_block(small_first), small_block(small_second)
    extra = jnp.where(is_first, block_first, block_second)
    extra_sent = jnp.where(is_first, block_second, block_first).astype(BF16)

    cd_first = near_in(kept_first[2], grad_cd)
    extra = extra + turned(extra_sent, "section", 1).astype(F32)
    sums_gate = SeqSum(gate_first).move()
    sums_out.scatter()
    cd_first.sent, sums_out.split = together(cd_first.sent, sums_out.split)
    sums_second.swap()
    cd_first.add_section()
    cd_first.blocks = [
        jnp.concatenate([block, extra.astype(BF16)], axis=0) for block in cd_first.blocks
    ]
    sums_second.own, cd_first.blocks = together(sums_second.own, cd_first.blocks)
    got_blocks = [turned(block, "wshard", away) for away, block in enumerate(cd_first.blocks, 1)]
    late = jnp.concatenate([cd_first.kept(0), extra], axis=0)
    late = (late + sum(block.astype(F32) for block in got_blocks)).astype(BF16)
    sums_gate.scatter()
    second = sums_second.whole()
    late, second, sums_gate.split = together(late, second, sums_gate.split)
    late = SeqSum(late).move()
    sums_out.gather()
    late.moving, sums_out.copies = together(late.moving, sums_out.copies)
    late.scatter()
    in_grad = placed_grads(grad_source, grad_middle_low)
    sums_out.swap()
    sums_out.own, late.split, in_grad = together(sums_out.own, late.split, in_grad)
    sums_gate.gather()
    late.gather()
    late.copies, sums_gate.copies = together(late.copies, sums_gate.copies)
    out_and_cd = sums_out.whole()
    sums_gate.swap()
    pick = section.astype(jnp.int32).reshape(1)

    def crossed(block, route):
        return [block, lax.ppermute(block, "section", route)]

    known = crossed(out_and_cd, [(0, 1), (1, 0)]) + crossed(second, [(0, 1)])
    (part_out,) = call(place_out_kernel, [((DI // shards, D), F32)], [], pick, *known)
    late.moving, part_out, known = together(late.moving, part_out, known)
    late.swap()
    gate_first, late_first = sums_gate.whole(), late.whole()
    (part_in,) = call(
        place_kernel,
        [((DI + DCD, 2 * lanes), F32)],
        [],
        pick,
        *crossed(gate_first, [(1, 0)]),
        *crossed(late_first, [(1, 0)]),
        *known,
    )
    mine = late_first[DCD:].astype(F32).reshape(-1)
    small_out, at = [], 0
    for part, shown in zip(small_first, small_parts):
        piece = mine[at : at + part.size].reshape(part.shape)
        at += part.size
        width = shown.shape[-1]
        piece = lax.dynamic_slice_in_dim(piece, shard * width, width, piece.ndim - 1)
        small_out.append(piece.reshape(shown.shape))
    return (
        acts,
        in_grad,
        small_out[0],
        jnp.swapaxes(part_in, 0, 1)[None],
        *small_out[1:],
        part_out[None],
    )


def solution(mesh):
    placed = (
        P(None, "wshard", "seq", None),
        P(None, "wshard", "seq", None),
        P(None, "wshard"),
        P("section", "wshard"),
        P("section", "wshard", None),
        P("section", None, "wshard"),
        P("section", "wshard"),
        P("section", "wshard"),
        P("section", "wshard"),
        P("section", "wshard"),
        P("section", "wshard"),
        P("section", "wshard", None),
    )
    return jax.shard_map(
        on_device,
        mesh=mesh,
        in_specs=placed,
        out_specs=(
            P("section", None, "wshard", "seq", None),
            P("section", None, "wshard", "seq", None),
            P("section", "wshard"),
            P("section", "wshard", None),
            P("section", None, "wshard"),
            P("section", "wshard"),
            P("section", "wshard"),
            P("section", "wshard"),
            P("section", "wshard"),
            P("section", "wshard"),
            P("section", "wshard", None),
        ),
        check_vma=False,
    )
```
